128 devices in a mesh: phase: 4 (over x_hi, core), tile: 32 (over x_lo, z, y).
Axes of the slice: x: 4 (x_hi: 2, x_lo: 2; x = x_hi * 2 + x_lo), y: 4, z: 4, core: 2. Of those that a mesh axis runs over, the one named last changes fastest.
Arguments:
- adjoint_in: float32 [16, 4, 256, 128, 128], P('phase', None, 'tile'), may hold values from -6 to 6
- velocity: bfloat16 [16, 3, 256, 128, 128], P('phase', None, 'tile'), may hold values from -4 to 4
- temp_grad: bfloat16 [16, 3, 256, 128, 128], P('phase', None, 'tile'), may hold values from -3 to 3
- heat_weight: bfloat16 [16, 256, 128, 128], P('phase', 'tile'), may hold values from -6 to 6
- density: float32 [256, 128, 128], P('tile'), may hold values from 0.02 to 1
- cell_kind: int32 [256, 128, 128], P('tile'), may hold values from 0 to 2
- inlet: int32 [256, 128, 128], P('tile'), may hold values 0 or 1
Outputs:
- adjoint_out: float32 [16, 4, 256, 128, 128], P('phase', None, 'tile')
- sensitivity: float32 [256, 128, 128], P('tile')
The draws below stay inside these ranges and needn't reach their ends.
All inputs are finite; a program needn't handle non-finite values. No bound on the sum of `inlet` on one device may be relied on, other than what follows from the above.
Results may differ from the reference program's by a relative error of at most 0.0003.
Values may be sent and summed in bfloat16 or wider, within the bound.
A program may use at most 320 MiB of HBM per device.

```python
import jax
import jax.numpy as jnp
from jax import lax

CX = 128
CZ = 128
STEPS = 3
NT = 16
NY = 256


def plant(drawn, rng, least, largest):
    index_at = [jax.random.randint(jax.random.fold_in(rng, axis), (), 0, length) for axis, length in enumerate(drawn.shape)]
    longest = drawn.shape.index(max(drawn.shape))
    next_to = index_at[:longest] + [(index_at[longest] + 1) % drawn.shape[longest]] + index_at[longest + 1:]
    return drawn.at[tuple(index_at)].set(least).at[tuple(next_to)].set(largest)


def steps_of(own_key, extent, cuts, least, largest):
    def one(position, parts):
        heights = jax.random.uniform(jax.random.fold_in(jax.random.fold_in(own_key, 6), position), (parts,), jnp.float32, least / len(cuts), largest / len(cuts))
        return jnp.repeat(jnp.exp(heights), extent[position] // parts).reshape((-1,) + (1,) * (len(extent) - position - 1))

    level = one(*cuts[0])
    for cut in cuts[1:]:
        level = level * one(*cut)
    return level


def scatter_about(own_key, extent, spread, bound, shards=(), kind=jnp.bfloat16):
    factor_of = steps_of(own_key, extent, shards, -0.22, 0.18) if shards else 1.0
    values = jax.random.normal(own_key, extent, jnp.float32) * spread * factor_of
    return jnp.minimum(jnp.maximum(values, -bound), bound).astype(kind)


def setup_inputs(seed: int = 0) -> dict:
    key_of = jax.random.split(jax.random.key(seed), 8)
    return {
        "adjoint_in": scatter_about(key_of[0], (NT, 4, NY, CX, CZ), 1.0, 6.0, ((0, 4), (2, 32)), jnp.float32),
        "velocity": scatter_about(key_of[1], (NT, 3, NY, CX, CZ), 1.0, 4.0, ((0, 4), (2, 32))),
        "temp_grad": scatter_about(key_of[2], (NT, 3, NY, CX, CZ), 0.5, 3.0, ((0, 4), (2, 32))),
        "heat_weight": scatter_about(key_of[3], (NT, NY, CX, CZ), 1.0, 6.0, ((0, 4), (1, 32))),
        "density": jnp.clip(0.02 + 0.98 * jax.random.uniform(key_of[4], (NY, CX, CZ), jnp.float32) ** steps_of(key_of[4], (NY, CX, CZ), ((0, 32),), -0.2, 0.2), 0.02, 1.0),
        "cell_kind": plant(jax.random.randint(key_of[5], (NY, CX, CZ), 0, 3), jax.random.fold_in(key_of[5], 1), 0, 2).astype(jnp.int32),
        "inlet": plant((jax.random.randint(key_of[6], (NY, CX, CZ), 0, 16) < 1).astype(jnp.int32), jax.random.fold_in(key_of[6], 1), 0, 1),
    }


def coefficients(density, cell_kind):
    rho = jnp.where(cell_kind == 0, density, jnp.where(cell_kind == 2, jnp.ones_like(density), jnp.zeros_like(density)))
    penalty = 0.5 * 0.5 * (1.0 - rho) / (0.5 + rho)
    slope = jnp.where(cell_kind == 0, -0.5 * 0.5 * 1.5 / ((0.5 + rho) * (0.5 + rho)), jnp.zeros_like(rho))
    return penalty, slope


def advance(extended, flow, temp_grad, heat, penalty, keep):
    center = extended[..., 1:-1, :, :]
    lower = extended[..., :-2, :, :]
    upper = extended[..., 2:, :, :]
    widths = [(0, 0)] * (center.ndim - 2) + [(1, 1), (1, 1)]
    padded = jnp.pad(center, widths)
    left = padded[..., :-2, 1:-1]
    right = padded[..., 2:, 1:-1]
    below = padded[..., 1:-1, :-2]
    above = padded[..., 1:-1, 2:]
    laplace = upper + lower + left + right + below + above - 6.0 * center
    momentum = center[..., 0:3, :, :, :]
    thermal = center[..., 3, :, :, :]
    grad_x = 0.5 * (right - left)[..., 3, :, :, :]
    grad_y = 0.5 * (upper - lower)[..., 3, :, :, :]
    grad_z = 0.5 * (above - below)[..., 3, :, :, :]
    speed = flow.astype(jnp.float32)
    advect = speed[..., 0, :, :, :] * grad_x + speed[..., 1, :, :, :] * grad_y + speed[..., 2, :, :, :] * grad_z
    coupling = jnp.expand_dims(thermal, -4) * temp_grad.astype(jnp.float32)
    mom_new = keep * (momentum + 0.12 * laplace[..., 0:3, :, :, :] - penalty * momentum - coupling)
    heat_new = thermal + 0.12 * laplace[..., 3, :, :, :] + 0.2 * advect + heat.astype(jnp.float32)
    return jnp.concatenate([mom_new, jnp.expand_dims(heat_new, -4)], axis=-4)


def reference(adjoint_in, velocity, temp_grad, heat_weight, density, cell_kind, inlet):
    penalty, slope = coefficients(density, cell_kind)
    keep = (1 - inlet).astype(density.dtype)
    phases = adjoint_in.shape[0]
    state = adjoint_in
    for step in range(STEPS):
        def one_phase(items, current=state):
            index, flow, grads, heat = items
            later = lax.dynamic_index_in_dim(current, (index + 1) % phases, 0, keepdims=False)
            extended = jnp.pad(later, ((0, 0), (1, 1), (0, 0), (0, 0)))
            return advance(extended, flow, grads, heat, penalty, keep)
        state = lax.map(one_phase, (jnp.arange(phases, dtype=jnp.int32), velocity, temp_grad, heat_weight))
    terms = jnp.sum(velocity.astype(jnp.float32) * state[:, 0:3], axis=(0, 1))
    return state, slope * terms
```

```python
import functools

import jax
import jax.numpy as jnp
from jax import lax
from jax.experimental import pallas as pl
from jax.experimental.pallas import tpu as pltpu
from jax.sharding import PartitionSpec as P

F32 = jnp.float32
PAD = 8
BLOCK = 32
TOP = 32767.0
MESH = pl.DeviceIdType.MESH


def rho_of(density, kind):
    return jnp.where(kind == 0, density, jnp.where(kind == 2, 1.0, 0.0))


def kernel(
    tiles, adj, vel, grad, heat, density, kind, inlet, out, sens,
    state, fin, v_buf, g_buf, w_buf, d_buf, k_buf, i_buf, cen, nbr, keep, acc, half, part, whole,
    xs_q, xs_s, xr_q, xr_s, hs_q, hs_s, hr_q, hr_s,
    load_sem, out_sem, x_send, x_recv, h_send, h_recv, s_send, s_recv,
):
    ny, nx, nz = d_buf.shape
    group, tile = lax.axis_index("phase"), lax.axis_index("tile")
    core = lax.rem(group, 2)
    before, after, across = (lax.rem(group + n, 4) for n in (3, 1, 2))
    partner = group + 1 - 2 * core
    has_down, has_up = tile > 0, tile < tiles - 1
    body = pl.ds(PAD, nx)

    loads = {}

    def load(name, number, src, dst):
        loads[name] = pltpu.make_async_copy(src, dst, load_sem.at[number])
        loads[name].start()

    for t in range(4):
        load(f"s{t}", t, adj.at[t], state.at[t, :, pl.ds(1, ny), body, :])
    load("density", 4, density, d_buf)
    load("kind", 5, kind, k_buf)
    load("inlet", 6, inlet, i_buf)
    for t in (0, 1, 2, 3):
        load(f"v{t}", 7 + 3 * t, vel.at[t], v_buf.at[t])
        load(f"g{t}", 8 + 3 * t, grad.at[t], g_buf.at[t])
        load(f"w{t}", 9 + 3 * t, heat.at[t], w_buf.at[t])

    edge = jnp.zeros((PAD, nz), F32)

    def clear(y, carry):
        for slot in range(state.shape[0]):
            for c in range(4):
                state[slot, c, y, 0:PAD, :] = edge
                state[slot, c, y, PAD + nx : 2 * PAD + nx, :] = edge
        return carry

    lax.fori_loop(0, ny + 2, clear, 0)

    barrier = pltpu.get_barrier_semaphore()
    for other in (before, after, across):
        pl.semaphore_signal(barrier, 1, device_id=(other, tile), device_id_type=MESH)

    @pl.when(has_down)
    def _():
        pl.semaphore_signal(barrier, 1, device_id=(group, tile - 1), device_id_type=MESH)

    @pl.when(has_up)
    def _():
        pl.semaphore_signal(barrier, 1, device_id=(group, tile + 1), device_id_type=MESH)

    pl.semaphore_wait(barrier, 3 + has_down.astype(jnp.int32) + has_up.astype(jnp.int32))

    def encode(slot, y, q, s):
        for c in range(4):
            v = state[slot, c, y + 1, PAD : PAD + nx, :]
            top = jnp.maximum(jnp.max(jnp.abs(v), axis=0, keepdims=True), 1e-30)
            q[c] = jnp.round(v * (TOP / top)).astype(jnp.int32).astype(jnp.int16)
            scale = top * (1.0 / TOP)
            s[c : c + 1, :] = scale
            s[c + 4 : c + 5, :] = scale

    def decode(q, s, slot, row):
        for c in range(4):
            code = q[c].astype(jnp.int32).astype(F32)
            state[slot, c, row, PAD : PAD + nx, :] = code * s[c : c + 1, :]

    def crossing(u, y):
        return [
            pltpu.make_async_remote_copy(
                a.at[u, y], b.at[u, y], x_send.at[u, y, n], x_recv.at[u, y, n],
                device_id=(before, tile), device_id_type=MESH,
            )
            for n, (a, b) in enumerate(((xs_q, xr_q), (xs_s, xr_s)))
        ]

    def cross(u, slot, y):
        encode(slot, y, xs_q.at[u, y], xs_s.at[u, y])
        for copy in crossing(u, y):
            copy.start()

    def halo(u, side, q, s):
        other = tile + 1 - 2 * side
        return [
            pltpu.make_async_remote_copy(
                a, b.at[u, side], h_send.at[u, side, n], h_recv.at[u, side, n],
                device_id=(group, other), device_id_type=MESH,
            )
            for n, (a, b) in enumerate(((q, hr_q), (s, hr_s)))
        ]

    def offer(u, slot):
        for side, there, y in ((0, has_up, ny - 1), (1, has_down, 0)):

            @pl.when(there)
            def _():
                encode(slot, y, hs_q.at[u, side], hs_s.at[u, side])
                for copy in halo(u, side, hs_q.at[u, side], hs_s.at[u, side]):
                    copy.start()

    def relay(u, x):
        for side, there, y in ((0, has_up, ny - 1), (1, has_down, 0)):
            for copy in crossing(x, y):
                copy.wait_recv()

            @pl.when(there)
            def _():
                for copy in halo(u, side, xr_q.at[x, y], xr_s.at[x, y]):
                    copy.start()

    def take_halo(u, slot):
        for side, there, row in ((0, has_down, 0), (1, has_up, ny + 1)):

            @pl.when(there)
            def _():
                for copy in halo(u, side, hs_q.at[u, side], hs_s.at[u, side]):
                    copy.wait_recv()
                decode(hr_q.at[u, side], hr_s.at[u, side], slot, row)

            @pl.when(jnp.logical_not(there))
            def _():
                for c in range(4):
                    state[slot, c, row, PAD : PAD + nx, :] = jnp.zeros((nx, nz), F32)

    def take_plane(x, slot, y, wait):
        if wait:
            for copy in crossing(x, y):
                copy.wait_recv()
        decode(xr_q.at[x, y], xr_s.at[x, y], slot, y + 1)

    lane = lax.broadcasted_iota(jnp.int32, (BLOCK, nz), 1)
    not_first, not_last = lane > 0, lane < nz - 1

    def plane(slot, t, y, target, total):
        for x0 in range(0, nx, BLOCK):
            rows = slice(PAD + x0, PAD + x0 + BLOCK)
            left = slice(PAD + x0 - 1, PAD + x0 + BLOCK - 1)
            right = slice(PAD + x0 + 1, PAD + x0 + BLOCK + 1)
            here = slice(x0, x0 + BLOCK)

            def around(c):
                mid = state[slot, c, y + 1, rows, :]
                below = jnp.where(not_first, pltpu.roll(mid, 1, 1), 0.0)
                above = jnp.where(not_last, pltpu.roll(mid, nz - 1, 1), 0.0)
                return (
                    mid, state[slot, c, y + 1, left, :], state[slot, c, y + 1, right, :],
                    state[slot, c, y, rows, :], state[slot, c, y + 2, rows, :], below, above,
                )

            h, xl, xr, yl, yu, zl, zr = around(3)
            speed = [v_buf[t, c, y, here, :].astype(F32) for c in range(3)]
            turn = speed[0] * (xr - xl) + speed[1] * (yu - yl) + speed[2] * (zr - zl)
            ring = (xl + xr) + (yl + yu) + (zl + zr)
            h_new = 0.28 * h + 0.12 * ring + 0.1 * turn + w_buf[t, y, here, :].astype(F32)
            put(target, 3, y, x0, h_new)
            kh = keep[y, here, :] * h
            a, b = cen[y, here, :], nbr[y, here, :]
            term = None
            for c in range(3):
                m, xl, xr, yl, yu, zl, zr = around(c)
                ring = (xl + xr) + (yl + yu) + (zl + zr)
                new = a * m + b * ring - kh * g_buf[t, c, y, here, :].astype(F32)
                put(target, c, y, x0, new)
                if total is not None:
                    term = speed[c] * new if term is None else term + speed[c] * new
            if total == "set":
                acc[y, here, :] = term
            elif total == "add":
                acc[y, here, :] = acc[y, here, :] + term

    def put(target, c, y, x0, value):
        kind_of, number = target
        if kind_of == "fin":
            fin[number, c, y, x0 : x0 + BLOCK, :] = value
        else:
            state[number, c, y + 1, PAD + x0 : PAD + x0 + BLOCK, :] = value

    def out_copy(t, y):
        return pltpu.make_async_copy(fin.at[t, :, y], out.at[t, :, y], out_sem.at[t, y])

    def chain(slot, t, target, halo_out=None, cross_out=None, total=None):
        def one(i, carry):
            y = lax.rem(i + ny - 1, ny)
            plane(slot, t, y, target, total)
            if cross_out is not None:
                cross(cross_out, target[1], y)
            if target[0] == "fin":
                out_copy(t, y).start()
            if halo_out is not None:

                @pl.when(i == 1)
                def _():
                    offer(halo_out, target[1])

            return carry

        lax.fori_loop(0, ny, one, 0)

    def take_crossing(x, slot):
        def one(i, carry):
            take_plane(x, slot, i, True)
            return carry

        lax.fori_loop(1, ny - 1, one, 0)
        take_plane(x, slot, 0, False)
        take_plane(x, slot, ny - 1, False)

    loads["s0"].wait()

    def first(i, carry):
        cross(0, 0, lax.rem(i + ny - 1, ny))
        return carry

    lax.fori_loop(0, ny, first, 0)
    for t in (1, 2, 3):
        loads[f"s{t}"].wait()
        offer(t - 1, t)

    for name in ("density", "kind", "inlet"):
        loads[name].wait()

    def prepare(y, carry):
        rho = rho_of(d_buf[y], k_buf[y])
        under = 1.0 / (0.5 + rho)
        open_ = (1 - i_buf[y]).astype(F32)
        keep[y] = open_
        nbr[y] = 0.12 * open_
        cen[y] = open_ * (0.28 - 0.25 * (1.0 - rho) * under)
        d_buf[y] = jnp.where(k_buf[y] == 0, -0.375 * under * under, 0.0)
        return carry

    lax.fori_loop(0, ny, prepare, 0)

    def ready(t):
        for n in "vgw":
            loads[f"{n}{t}"].wait()

    S = "state"
    ready(0)
    take_halo(0, 1)
    chain(1, 0, (S, 4), cross_out=1)
    ready(1)
    take_halo(1, 2)
    chain(2, 1, (S, 5), halo_out=3)
    relay(4, 0)
    ready(2)
    take_halo(2, 3)
    chain(3, 2, (S, 1), halo_out=5)
    take_halo(3, 5)
    chain(5, 0, (S, 4), cross_out=2)
    ready(3)
    take_crossing(0, 0)
    take_halo(4, 0)
    chain(0, 3, (S, 3), halo_out=6)
    take_halo(5, 1)
    chain(1, 1, (S, 2), halo_out=7)
    relay(8, 1)
    take_halo(6, 3)
    chain(3, 2, (S, 1), halo_out=9)
    take_halo(7, 2)
    chain(2, 0, ("fin", 0), total="set")
    take_halo(9, 1)
    chain(1, 1, ("fin", 1), total="add")
    take_crossing(1, 0)
    take_halo(8, 0)
    chain(0, 3, (S, 4), halo_out=10)
    relay(11, 2)
    take_halo(10, 4)
    chain(4, 2, ("fin", 2), total="add")
    take_crossing(2, 5)
    take_halo(11, 5)
    chain(5, 3, ("fin", 3), total="add")

    mine, theirs = pl.ds(core * (ny // 2), ny // 2), pl.ds((1 - core) * (ny // 2), ny // 2)

    def send(n, src, dst, other):
        return pltpu.make_async_remote_copy(
            src, dst, s_send.at[n], s_recv.at[n], device_id=(other, tile), device_id_type=MESH
        )

    swap = send(0, acc.at[theirs], part.at[0], partner)
    swap.start()
    swap.wait_recv()
    half[...] = acc[mine] + part[0]
    far = send(1, half, part.at[1], across)
    far.start()
    far.wait_recv()
    whole[mine] = half[...] + part[1]
    back = send(2, whole.at[mine], whole.at[mine], partner)
    back.start()
    swap.wait_send()
    send(2, whole.at[theirs], whole.at[theirs], partner).wait_recv()
    far.wait_send()
    back.wait_send()
    acc[...] = d_buf[...] * whole[...]
    last = pltpu.make_async_copy(acc, sens, load_sem.at[0])
    last.start()

    def settle(y, carry):
        for u in range(3):
            for copy in crossing(u, y):
                copy.wait_send()
        for t in range(4):
            out_copy(t, y).wait()
        return carry

    lax.fori_loop(0, ny, settle, 0)
    for side, there in ((0, has_up), (1, has_down)):

        @pl.when(there)
        def _():
            for u in range(12):
                for copy in halo(u, side, hs_q.at[u, side], hs_s.at[u, side]):
                    copy.wait_send()

    last.wait()


def on_device(tiles, adjoint_in, velocity, temp_grad, heat_weight, density, cell_kind, inlet):
    phases, _, ny, nx, nz = adjoint_in.shape
    bf16, i16, i32 = jnp.bfloat16, jnp.int16, jnp.int32
    vmem, dma = pltpu.VMEM, pltpu.SemaphoreType.DMA
    return pl.pallas_call(
        functools.partial(kernel, tiles),
        out_shape=(
            jax.ShapeDtypeStruct(adjoint_in.shape, F32),
            jax.ShapeDtypeStruct(density.shape, F32),
        ),
        in_specs=[pl.BlockSpec(memory_space=pl.ANY)] * 7,
        out_specs=[pl.BlockSpec(memory_space=pl.ANY)] * 2,
        scratch_shapes=[
            vmem((6, 4, ny + 2, nx + 2 * PAD, nz), F32),
            vmem((phases, 4, ny, nx, nz), F32),
            vmem((phases, 3, ny, nx, nz), bf16),
            vmem((phases, 3, ny, nx, nz), bf16),
            vmem((phases, ny, nx, nz), bf16),
            vmem((ny, nx, nz), F32),
            vmem((ny, nx, nz), i32),
            vmem((ny, nx, nz), i32),
            vmem((ny, nx, nz), F32),
            vmem((ny, nx, nz), F32),
            vmem((ny, nx, nz), F32),
            vmem((ny, nx, nz), F32),
            vmem((ny // 2, nx, nz), F32),
            vmem((2, ny // 2, nx, nz), F32),
            vmem((ny, nx, nz), F32),
            vmem((3, ny, 4, nx, nz), i16),
            vmem((3, ny, 8, nz), F32),
            vmem((3, ny, 4, nx, nz), i16),
            vmem((3, ny, 8, nz), F32),
            vmem((12, 2, 4, nx, nz), i16),
            vmem((12, 2, 8, nz), F32),
            vmem((12, 2, 4, nx, nz), i16),
            vmem((12, 2, 8, nz), F32),
            dma((19,)),
            dma((phases, ny)),
            dma((3, ny, 2)),
            dma((3, ny, 2)),
            dma((12, 2, 2)),
            dma((12, 2, 2)),
            dma((3,)),
            dma((3,)),
        ],
        compiler_params=pltpu.CompilerParams(
            collective_id=0, has_side_effects=True, vmem_limit_bytes=60 * 2**20
        ),
    )(adjoint_in, velocity, temp_grad, heat_weight, density, cell_kind, inlet)


def solution(mesh):
    return jax.shard_map(
        functools.partial(on_device, mesh.shape["tile"]),
        mesh=mesh,
        in_specs=(
            P("phase", None, "tile", None, None),
            P("phase", None, "tile", None, None),
            P("phase", None, "tile", None, None),
            P("phase", "tile", None, None),
            P("tile", None, None),
            P("tile", None, None),
            P("tile", None, None),
        ),
        out_specs=(P("phase", None, "tile", None, None), P("tile", None, None)),
        check_vma=False,
    )
```

```python
import functools

import jax
import jax.numpy as jnp
from jax import lax
from jax.experimental import pallas as pl
from jax.experimental.pallas import tpu as pltpu
from jax.sharding import PartitionSpec as P

F32 = jnp.float32
PAD = 8
BLOCK = 32
TOP = 32767.0
MESH = pl.DeviceIdType.MESH


def rho_of(density, kind):
    return jnp.where(kind == 0, density, jnp.where(kind == 2, 1.0, 0.0))


def kernel(
    tiles, adj, vel, grad, heat, density, kind, inlet, out, sens,
    state, fin, v_buf, g_buf, w_buf, d_buf, k_buf, i_buf, cen, nbr, keep, acc, half, near, far, whole,
    xs_q, xs_s, xr_q, xr_s, hs_q, hs_s, hr_q, hr_s, via_q,
    load_sem, out_sem, x_send, x_recv, h_send, h_recv, s_send, s_recv, via_send, via_recv,
):
    ny, nx, nz = d_buf.shape
    group, tile = lax.axis_index("phase"), lax.axis_index("tile")
    core = lax.rem(group, 2)
    lower = 1 - tile // (tiles // 2)
    place = lower * tile + (1 - lower) * (tiles - 1 - tile)
    vias = (0, 3, 12)
    via = (place == vias[0]) | (place == vias[1]) | (place == vias[2])
    via_part = 1 + place // 3 - 2 * (place // 12)
    meets = place == tiles // 2 - 1
    lower_end, upper_end = tiles // 2 - 1, tiles // 2
    via_from = lower * lower_end + (1 - lower) * upper_end
    via_to = tiles - 1 - via_from
    before, after, across = (lax.rem(group + n, 4) for n in (3, 1, 2))
    partner = group + 1 - 2 * core
    has_down, has_up = tile > 0, tile < tiles - 1
    body = pl.ds(PAD, nx)

    loads = {}

    def load(name, number, src, dst):
        loads[name] = pltpu.make_async_copy(src, dst, load_sem.at[number])
        loads[name].start()

    def load_state(t):
        load(f"s{t}", t, adj.at[t], state.at[t, :, pl.ds(1, ny), body, :])

    def load_flow(t):
        load(f"v{t}", 7 + 3 * t, vel.at[t], v_buf.at[t])
        load(f"g{t}", 8 + 3 * t, grad.at[t], g_buf.at[t])
        load(f"w{t}", 9 + 3 * t, heat.at[t], w_buf.at[t])

    load_state(0)
    load_state(1)
    load_state(2)
    load("density", 4, density, d_buf)
    load("kind", 5, kind, k_buf)
    load("inlet", 6, inlet, i_buf)
    load_flow(0)
    load_state(3)
    for t in (1, 2, 3):
        load_flow(t)

    edge = jnp.zeros((PAD, nz), F32)

    def clear(y, carry):
        for slot in range(state.shape[0]):
            for c in range(4):
                state[slot, c, y, 0:PAD, :] = edge
                state[slot, c, y, PAD + nx : 2 * PAD + nx, :] = edge
        return carry

    lax.fori_loop(0, ny + 2, clear, 0)

    barrier = pltpu.get_barrier_semaphore()
    for other in (before, after, across):
        pl.semaphore_signal(barrier, 1, device_id=(other, tile), device_id_type=MESH)

    @pl.when(has_down)
    def _():
        pl.semaphore_signal(barrier, 1, device_id=(group, tile - 1), device_id_type=MESH)

    @pl.when(has_up)
    def _():
        pl.semaphore_signal(barrier, 1, device_id=(group, tile + 1), device_id_type=MESH)

    @pl.when(via)
    def _():
        pl.semaphore_signal(barrier, 1, device_id=(group, via_from), device_id_type=MESH)

    @pl.when(meets)
    def _():
        for v in vias:
            other = (1 - lower) * v + lower * (tiles - 1 - v)
            pl.semaphore_signal(barrier, 1, device_id=(group, other), device_id_type=MESH)

    extra = via.astype(jnp.int32) + 3 * meets.astype(jnp.int32)
    pl.semaphore_wait(barrier, 3 + has_down.astype(jnp.int32) + has_up.astype(jnp.int32) + extra)

    def encode(slot, y, q, s):
        for c in range(4):
            v = state[slot, c, y + 1, PAD : PAD + nx, :]
            top = jnp.maximum(jnp.max(jnp.abs(v), axis=0, keepdims=True), 1e-30)
            q[c] = jnp.round(v * (TOP / top)).astype(jnp.int32).astype(jnp.int16)
            scale = top * (1.0 / TOP)
            s[c : c + 1, :] = scale
            s[c + 4 : c + 5, :] = scale

    def decode(q, s, slot, row):
        for c in range(4):
            code = q[c].astype(jnp.int32).astype(F32)
            state[slot, c, row, PAD : PAD + nx, :] = code * s[c : c + 1, :]

    def crossing(u, y):
        return [
            pltpu.make_async_remote_copy(
                a.at[u, y], b.at[u, y], x_send.at[u, y, n], x_recv.at[u, y, n],
                device_id=(before, tile), device_id_type=MESH,
            )
            for n, (a, b) in enumerate(((xs_q, xr_q), (xs_s, xr_s)))
        ]

    order = iter([(u, (i + ny - 1) % ny) for u in range(3) for i in range(ny)])

    def cross(u, y):
        for copy in crossing(u, y):
            copy.start()

    def encode_crossing(u, slot, y):
        encode(slot, y, xs_q.at[u, y], xs_s.at[u, y])

    def halo(u, side, q, s):
        other = tile + 1 - 2 * side
        return [
            pltpu.make_async_remote_copy(
                a, b.at[u, side], h_send.at[u, side, n], h_recv.at[u, side, n],
                device_id=(group, other), device_id_type=MESH,
            )
            for n, (a, b) in enumerate(((q, hr_q), (s, hr_s)))
        ]

    def post(u, side, q, s):
        number, scale = halo(u, side, q, s)
        far_apart = tile == (lower_end, upper_end)[side]

        @pl.when(jnp.logical_not(far_apart))
        def _():
            number.start()

        @pl.when(far_apart)
        def _():
            pltpu.make_async_remote_copy(
                q.at[0], hr_q.at[u, side, 0], h_send.at[u, side, 0], h_recv.at[u, side, 0],
                device_id=(group, tile + 1 - 2 * side), device_id_type=MESH,
            ).start()
            for c, v in enumerate(vias, 1):
                pltpu.make_async_remote_copy(
                    q.at[c], via_q.at[u], h_send.at[u, side, 0], via_recv.at[u],
                    device_id=(group, (v, tiles - 1 - v)[side]), device_id_type=MESH,
                ).start()

        scale.start()

    def passed_on(u):
        return pltpu.make_async_remote_copy(
            via_q.at[u], hr_q.at[u, 1 - lower, via_part], via_send.at[u], h_recv.at[u, 1 - lower, 0],
            device_id=(group, via_to), device_id_type=MESH,
        )

    def pass_on(*units):
        @pl.when(via)
        def _():
            for u in units:
                pltpu.make_async_remote_copy(
                    via_q.at[u], via_q.at[u], via_send.at[u], via_recv.at[u],
                    device_id=(group, via_to), device_id_type=MESH,
                ).wait_recv()
                passed_on(u).start()

    def offer(u, slot):
        for side, there, y in ((0, has_up, ny - 1), (1, has_down, 0)):

            @pl.when(there)
            def _():
                encode(slot, y, hs_q.at[u, side], hs_s.at[u, side])
                post(u, side, hs_q.at[u, side], hs_s.at[u, side])

    def relay(u, x):
        for side, there, y in ((0, has_up, ny - 1), (1, has_down, 0)):
            for copy in crossing(x, y):
                copy.wait_recv()

            @pl.when(there)
            def _():
                post(u, side, xr_q.at[x, y], xr_s.at[x, y])

    def take_halo(u, slot):
        for side, there, row in ((0, has_down, 0), (1, has_up, ny + 1)):

            @pl.when(there)
            def _():
                for copy in halo(u, side, hs_q.at[u, side], hs_s.at[u, side]):
                    copy.wait_recv()
                decode(hr_q.at[u, side], hr_s.at[u, side], slot, row)

            @pl.when(jnp.logical_not(there))
            def _():
                for c in range(4):
                    state[slot, c, row, PAD : PAD + nx, :] = jnp.zeros((nx, nz), F32)

    def take_plane(x, slot, y, wait):
        if wait:
            for copy in crossing(x, y):
                copy.wait_recv()
        decode(xr_q.at[x, y], xr_s.at[x, y], slot, y + 1)

    lane = lax.broadcasted_iota(jnp.int32, (BLOCK, nz), 1)
    not_first, not_last = lane > 0, lane < nz - 1

    def plane(slot, t, y, target, total):
        for x0 in range(0, nx, BLOCK):
            rows = slice(PAD + x0, PAD + x0 + BLOCK)
            left = slice(PAD + x0 - 1, PAD + x0 + BLOCK - 1)
            right = slice(PAD + x0 + 1, PAD + x0 + BLOCK + 1)
            here = slice(x0, x0 + BLOCK)

            def around(c):
                mid = state[slot, c, y + 1, rows, :]
                below = jnp.where(not_first, pltpu.roll(mid, 1, 1), 0.0)
                above = jnp.where(not_last, pltpu.roll(mid, nz - 1, 1), 0.0)
                return (
                    mid, state[slot, c, y + 1, left, :], state[slot, c, y + 1, right, :],
                    state[slot, c, y, rows, :], state[slot, c, y + 2, rows, :], below, above,
                )

            h, xl, xr, yl, yu, zl, zr = around(3)
            speed = [v_buf[t, c, y, here, :].astype(F32) for c in range(3)]
            turn = speed[0] * (xr - xl) + speed[1] * (yu - yl) + speed[2] * (zr - zl)
            ring = (xl + xr) + (yl + yu) + (zl + zr)
            h_new = 0.28 * h + 0.12 * ring + 0.1 * turn + w_buf[t, y, here, :].astype(F32)
            put(target, 3, y, x0, h_new)
            kh = keep[y, here, :] * h
            a, b = cen[y, here, :], nbr[y, here, :]
            term = None
            for c in range(3):
                m, xl, xr, yl, yu, zl, zr = around(c)
                ring = (xl + xr) + (yl + yu) + (zl + zr)
                new = a * m + b * ring - kh * g_buf[t, c, y, here, :].astype(F32)
                put(target, c, y, x0, new)
                if total is not None:
                    term = speed[c] * new if term is None else term + speed[c] * new
            if total == "set":
                acc[y, here, :] = term
            elif total == "add":
                acc[y, here, :] = acc[y, here, :] + term

    def put(target, c, y, x0, value):
        kind_of, number = target
        if kind_of == "fin":
            fin[number, c, y, x0 : x0 + BLOCK, :] = value
        else:
            state[number, c, y + 1, PAD + x0 : PAD + x0 + BLOCK, :] = value

    def out_copy(t, y):
        return pltpu.make_async_copy(fin.at[t, :, y], out.at[t, :, y], out_sem.at[t, y])

    def chain(slot, t, target, halo_out=None, cross_out=None, total=None, crosses=0):
        due = [next(order) for _ in range(crosses)]

        def one(i, carry):
            y = lax.rem(i + ny - 1, ny)
            plane(slot, t, y, target, total)
            if cross_out is not None:
                encode_crossing(cross_out, target[1], y)
            if target[0] == "fin":
                out_copy(t, y).start()
            if halo_out is not None:

                @pl.when(i == 1)
                def _():
                    offer(halo_out, target[1])

            for n, (u, plane_of) in enumerate(due):

                @pl.when(i == 2 + 2 * n)
                def _(u=u, plane_of=plane_of):
                    cross(u, plane_of)

            return carry

        lax.fori_loop(0, ny, one, 0)

    def take_crossing(x, slot):
        def one(i, carry):
            take_plane(x, slot, i, True)
            return carry

        lax.fori_loop(1, ny - 1, one, 0)
        take_plane(x, slot, 0, False)
        take_plane(x, slot, ny - 1, False)

    loads["s0"].wait()

    def first(i, carry):
        encode_crossing(0, 0, lax.rem(i + ny - 1, ny))
        return carry

    lax.fori_loop(0, ny, first, 0)
    for t in (1, 2, 3):
        loads[f"s{t}"].wait()
        offer(t - 1, t)
        if t == 1:
            cross(*next(order))
            cross(*next(order))

    for name in ("density", "kind", "inlet"):
        loads[name].wait()

    def prepare(y, carry):
        rho = rho_of(d_buf[y], k_buf[y])
        under = 1.0 / (0.5 + rho)
        open_ = (1 - i_buf[y]).astype(F32)
        keep[y] = open_
        nbr[y] = 0.12 * open_
        cen[y] = open_ * (0.28 - 0.25 * (1.0 - rho) * under)
        d_buf[y] = jnp.where(k_buf[y] == 0, -0.375 * under * under, 0.0)
        return carry

    lax.fori_loop(0, ny, prepare, 0)

    def ready(t):
        for n in "vgw":
            loads[f"{n}{t}"].wait()

    S = "state"
    pass_on(0, 1, 2)
    ready(0)
    take_halo(0, 1)
    chain(1, 0, (S, 4), cross_out=1, crosses=3)
    ready(1)
    take_halo(1, 2)
    chain(2, 1, (S, 5), halo_out=3, crosses=3)
    pass_on(3)
    relay(4, 0)
    ready(2)
    take_halo(2, 3)
    chain(3, 2, (S, 1), halo_out=5, crosses=3)
    pass_on(4, 5)
    take_halo(3, 5)
    chain(5, 0, (S, 4), cross_out=2, crosses=3)
    ready(3)
    take_crossing(0, 0)
    take_halo(4, 0)
    chain(0, 3, (S, 3), halo_out=6, crosses=2)
    pass_on(6)
    take_halo(5, 1)
    chain(1, 1, (S, 2), halo_out=7, crosses=3)
    pass_on(7)
    relay(8, 1)
    take_halo(6, 3)
    chain(3, 2, (S, 1), halo_out=9, crosses=3)
    pass_on(8, 9)
    take_halo(7, 2)
    chain(2, 0, ("fin", 0), total="set", crosses=2)
    take_halo(9, 1)
    chain(1, 1, ("fin", 1), total="add", crosses=0)
    take_crossing(1, 0)
    take_halo(8, 0)
    chain(0, 3, (S, 4), halo_out=10, crosses=0)
    pass_on(10)
    relay(11, 2)
    take_halo(10, 4)
    chain(4, 2, ("fin", 2), total="add", crosses=0)
    pass_on(11)

    def mine(k):
        return 2 * k + core

    def theirs(k):
        return 2 * k + 1 - core

    def send(n, k, src, dst, other):
        return pltpu.make_async_remote_copy(
            src, dst, s_send.at[n, k], s_recv.at[n, k], device_id=(other, tile), device_id_type=MESH
        )

    def to_partner(k):
        return send(0, k, acc.at[theirs(k)], near.at[k], partner)

    def to_other_chip(k):
        return send(1, k, half.at[k], far.at[k], across)

    def back(k, y):
        return send(2, k, whole.at[y], whole.at[y], partner)

    def sens_copy(y):
        return pltpu.make_async_copy(whole.at[y], sens.at[y], out_sem.at[4, y])

    def sum_chip(k):
        to_partner(k).wait_recv()
        half[k] = acc[mine(k)] + near[k]
        to_other_chip(k).start()

    def sum_all(k):
        to_other_chip(k).wait_recv()
        y = mine(k)
        whole[y] = d_buf[y] * (half[k] + far[k])
        back(k, y).start()
        sens_copy(y).start()

    take_halo(11, 5)
    take_plane(2, 5, 0, False)
    take_plane(2, 5, ny - 1, False)

    def last_pair(k, carry):
        @pl.when(k < ny // 2 - 1)
        def _():
            take_plane(2, 5, 2 * k + 1, True)
            take_plane(2, 5, 2 * k + 2, True)

        def one(y, carry):
            plane(5, 3, y, ("fin", 3), "add")
            out_copy(3, y).start()
            return carry

        lax.fori_loop(2 * k, 2 * k + 2, one, 0)
        to_partner(k).start()

        @pl.when(k > 0)
        def _():
            sum_chip(k - 1)

        @pl.when(k > 1)
        def _():
            sum_all(k - 2)

        return carry

    pairs = ny // 2
    lax.fori_loop(0, pairs, last_pair, 0)
    sum_chip(pairs - 1)
    sum_all(pairs - 2)
    sum_all(pairs - 1)
    for k in range(pairs):
        back(k, theirs(k)).wait_recv()
        sens_copy(theirs(k)).start()
    for k in range(pairs):
        to_partner(k).wait_send()
        to_other_chip(k).wait_send()
        back(k, mine(k)).wait_send()

    def settle(y, carry):
        for u in range(3):
            for copy in crossing(u, y):
                copy.wait_send()
        for t in range(4):
            out_copy(t, y).wait()
        sens_copy(y).wait()
        return carry

    lax.fori_loop(0, ny, settle, 0)
    for side, there in ((0, has_up), (1, has_down)):

        @pl.when(there)
        def _():
            for u in range(12):
                for copy in halo(u, side, hs_q.at[u, side], hs_s.at[u, side]):
                    copy.wait_send()

    @pl.when(via)
    def _():
        for u in range(12):
            passed_on(u).wait_send()


def hand_over(state, total, state_out, total_out, buf, into, onto):
    phases, ny = state.shape[0], state.shape[2]
    pieces = [(state.at[t, c], state_out.at[t, c]) for t in range(phases) for c in range(4)] + [(total, total_out)]
    ins = [pltpu.make_async_copy(a, buf.at[n], into.at[n]) for n, (a, _) in enumerate(pieces)]
    outs = [pltpu.make_async_copy(buf.at[n], b, onto.at[n]) for n, (_, b) in enumerate(pieces)]
    for copy in ins:
        copy.start()
    for a, b in zip(ins, outs, strict=True):
        a.wait()
        b.start()
    for copy in outs:
        copy.wait()


def on_device(tiles, adjoint_in, velocity, temp_grad, heat_weight, density, cell_kind, inlet):
    phases, _, ny, nx, nz = adjoint_in.shape
    bf16, i16, i32 = jnp.bfloat16, jnp.int16, jnp.int32
    vmem, dma = pltpu.VMEM, pltpu.SemaphoreType.DMA
    shapes = (
        jax.ShapeDtypeStruct(adjoint_in.shape, F32),
        jax.ShapeDtypeStruct(density.shape, F32),
    )
    anywhere = pl.BlockSpec(memory_space=pl.ANY)
    results = pl.pallas_call(
        functools.partial(kernel, tiles),
        out_shape=shapes,
        in_specs=[anywhere] * 7,
        out_specs=[anywhere] * 2,
        scratch_shapes=[
            vmem((6, 4, ny + 2, nx + 2 * PAD, nz), F32),
            vmem((phases, 4, ny, nx, nz), F32),
            vmem((phases, 3, ny, nx, nz), bf16),
            vmem((phases, 3, ny, nx, nz), bf16),
            vmem((phases, ny, nx, nz), bf16),
            vmem((ny, nx, nz), F32),
            vmem((ny, nx, nz), i32),
            vmem((ny, nx, nz), i32),
            vmem((ny, nx, nz), F32),
            vmem((ny, nx, nz), F32),
            vmem((ny, nx, nz), F32),
            vmem((ny, nx, nz), F32),
            vmem((ny // 2, nx, nz), F32),
            vmem((ny // 2, nx, nz), F32),
            vmem((ny // 2, nx, nz), F32),
            vmem((ny, nx, nz), F32),
            vmem((3, ny, 4, nx, nz), i16),
            vmem((3, ny, 8, nz), F32),
            vmem((3, ny, 4, nx, nz), i16),
            vmem((3, ny, 8, nz), F32),
            vmem((12, 2, 4, nx, nz), i16),
            vmem((12, 2, 8, nz), F32),
            vmem((12, 2, 4, nx, nz), i16),
            vmem((12, 2, 8, nz), F32),
            vmem((12, nx, nz), i16),
            dma((19,)),
            dma((phases + 1, ny)),
            dma((3, ny, 2)),
            dma((3, ny, 2)),
            dma((12, 2, 2)),
            dma((12, 2, 2)),
            dma((3, ny // 2)),
            dma((3, ny // 2)),
            dma((12,)),
            dma((12,)),
        ],
        compiler_params=pltpu.CompilerParams(
            collective_id=0, has_side_effects=True, vmem_limit_bytes=60 * 2**20
        ),
    )(adjoint_in, velocity, temp_grad, heat_weight, density, cell_kind, inlet)
    pieces = 4 * phases + 1
    return pl.pallas_call(
        hand_over,
        out_shape=shapes,
        in_specs=[pl.BlockSpec(memory_space=pltpu.HBM)] * 2,
        out_specs=[anywhere] * 2,
        scratch_shapes=[vmem((pieces, ny, nx, nz), F32), dma((pieces,)), dma((pieces,))],
        compiler_params=pltpu.CompilerParams(vmem_limit_bytes=60 * 2**20),
    )(*results)


def solution(mesh):
    return jax.shard_map(
        functools.partial(on_device, mesh.shape["tile"]),
        mesh=mesh,
        in_specs=(
            P("phase", None, "tile", None, None),
            P("phase", None, "tile", None, None),
            P("phase", None, "tile", None, None),
            P("phase", "tile", None, None),
            P("tile", None, None),
            P("tile", None, None),
            P("tile", None, None),
        ),
        out_specs=(P("phase", None, "tile", None, None), P("tile", None, None)),
        check_vma=False,
    )
```

```python
import functools
import math

import jax
import jax.numpy as jnp
from jax import lax
from jax.experimental import pallas as pl
from jax.experimental.pallas import tpu as pltpu
from jax.sharding import PartitionSpec as P

F32 = jnp.float32
PAD = 8
BLOCK = 32
TOP = 32767.0
TILE = 4096
MESH = pl.DeviceIdType.MESH


def rho_of(density, kind):
    return jnp.where(kind == 0, density, jnp.where(kind == 2, 1.0, 0.0))


def kernel(
    tiles, adj, vel, grad, heat, density, kind, inlet, out, sens,
    state, fin, v_buf, g_buf, w_buf, d_buf, k_buf, i_buf, cen, nbr, keep, acc, half, near, far, whole,
    xs_q, xs_s, xr_q, xr_s, hs_q, hs_s, hr_q, hr_s, via_q, tiles_of,
    load_sem, out_sem, x_send, x_recv, h_send, h_recv, s_send, s_recv, via_send, via_recv,
):
    ny, nx, nz = d_buf.shape
    group, tile = lax.axis_index("phase"), lax.axis_index("tile")
    core = lax.rem(group, 2)
    lower = 1 - tile // (tiles // 2)
    place = lower * tile + (1 - lower) * (tiles - 1 - tile)
    vias = (0, 3, 12)
    via = (place == vias[0]) | (place == vias[1]) | (place == vias[2])
    via_part = 1 + place // 3 - 2 * (place // 12)
    meets = place == tiles // 2 - 1
    lower_end, upper_end = tiles // 2 - 1, tiles // 2
    via_from = lower * lower_end + (1 - lower) * upper_end
    via_to = tiles - 1 - via_from
    before, after, across = (lax.rem(group + n, 4) for n in (3, 1, 2))
    partner = group + 1 - 2 * core
    has_down, has_up = tile > 0, tile < tiles - 1
    body = pl.ds(PAD, nx)

    loads = {}

    def load(name, number, *pairs):
        for src, dst in pairs:
            pltpu.make_async_copy(src, dst, load_sem.at[number]).start()
        loads[name] = (number, tiles_in(*(dst for _, dst in pairs)))

    def tiles_in(*refs):
        return sum(math.prod(r.shape) * jnp.dtype(r.dtype).itemsize for r in refs) // TILE

    def await_local(sem, n):
        pltpu.make_async_copy(tiles_of.at[pl.ds(0, n)], tiles_of.at[pl.ds(0, n)], sem).wait()

    def remote_bytes(sem, n):
        length = tiles_of.at[pl.ds(0, n)]
        return pltpu.make_async_remote_copy(
            length, length, sem, sem, device_id=(before, tile), device_id_type=MESH
        )

    packet = tiles_in(xs_q.at[0, 0], xs_s.at[0, 0])

    def loaded(name):
        number, size = loads[name]
        await_local(load_sem.at[number], size)

    def load_state(t):
        load(f"state {t}", t, (adj.at[t], state.at[t, :, pl.ds(1, ny), body, :]))

    def load_flow(t):
        here = ((vel.at[t], v_buf.at[t]), (grad.at[t], g_buf.at[t]), (heat.at[t], w_buf.at[t]))
        load(f"flow {t}", 5 + t, *here)

    load_state(2)
    load_state(0)

    edge = jnp.zeros((PAD, nz), F32)

    def clear(y, carry):
        for slot in range(state.shape[0]):
            for c in range(4):
                state[slot, c, y, 0:PAD, :] = edge
                state[slot, c, y, PAD + nx : 2 * PAD + nx, :] = edge
        return carry

    lax.fori_loop(0, ny + 2, clear, 0)

    barrier = pltpu.get_barrier_semaphore()
    for other in (before, after, across):
        pl.semaphore_signal(barrier, 1, device_id=(other, tile), device_id_type=MESH)

    @pl.when(has_down)
    def _():
        pl.semaphore_signal(barrier, 1, device_id=(group, tile - 1), device_id_type=MESH)

    @pl.when(has_up)
    def _():
        pl.semaphore_signal(barrier, 1, device_id=(group, tile + 1), device_id_type=MESH)

    @pl.when(via)
    def _():
        pl.semaphore_signal(barrier, 1, device_id=(group, via_from), device_id_type=MESH)

    @pl.when(meets)
    def _():
        for v in vias:
            other = (1 - lower) * v + lower * (tiles - 1 - v)
            pl.semaphore_signal(barrier, 1, device_id=(group, other), device_id_type=MESH)

    extra = via.astype(jnp.int32) + 3 * meets.astype(jnp.int32)
    pl.semaphore_wait(barrier, 3 + has_down.astype(jnp.int32) + has_up.astype(jnp.int32) + extra)

    def encode(slot, y, q, s):
        for c in range(4):
            v = state[slot, c, y + 1, PAD : PAD + nx, :]
            top = jnp.maximum(jnp.max(jnp.abs(v), axis=0, keepdims=True), 1e-30)
            q[c] = jnp.round(v * (TOP / top)).astype(jnp.int32).astype(jnp.int16)
            scale = top * (1.0 / TOP)
            s[c : c + 1, :] = scale
            s[c + 4 : c + 5, :] = scale

    def decode(q, s, slot, row):
        for c in range(4):
            code = q[c].astype(jnp.int32).astype(F32)
            state[slot, c, row, PAD : PAD + nx, :] = code * s[c : c + 1, :]

    def crossing(u, y):
        return [
            pltpu.make_async_remote_copy(
                a.at[u, y], b.at[u, y], x_send.at[0], x_recv.at[u, y],
                device_id=(before, tile), device_id_type=MESH,
            )
            for a, b in ((xs_q, xr_q), (xs_s, xr_s))
        ]

    order = iter([(u, (i + ny - 1) % ny) for u in range(3) for i in range(ny)])

    def cross(u, y):
        for copy in crossing(u, y):
            copy.start()

    def encode_crossing(u, slot, y):
        encode(slot, y, xs_q.at[u, y], xs_s.at[u, y])

    def halo(u, side, q, s):
        other = tile + 1 - 2 * side
        return [
            pltpu.make_async_remote_copy(
                a, b.at[side, u], h_send.at[side], h_recv.at[side, u],
                device_id=(group, other), device_id_type=MESH,
            )
            for a, b in ((q, hr_q), (s, hr_s))
        ]

    def post(u, side, q, s):
        number, scale = halo(u, side, q, s)
        far_apart = tile == (lower_end, upper_end)[side]

        @pl.when(jnp.logical_not(far_apart))
        def _():
            number.start()

        @pl.when(far_apart)
        def _():
            pltpu.make_async_remote_copy(
                q.at[0], hr_q.at[side, u, 0], h_send.at[side], h_recv.at[side, u],
                device_id=(group, tile + 1 - 2 * side), device_id_type=MESH,
            ).start()
            for c, v in enumerate(vias, 1):
                pltpu.make_async_remote_copy(
                    q.at[c], via_q.at[u], h_send.at[side], via_recv.at[u],
                    device_id=(group, (v, tiles - 1 - v)[side]), device_id_type=MESH,
                ).start()

        scale.start()

    def passed_on(u):
        return pltpu.make_async_remote_copy(
            via_q.at[u], hr_q.at[1 - lower, u, via_part], via_send.at[0], h_recv.at[1 - lower, u],
            device_id=(group, via_to), device_id_type=MESH,
        )

    def pass_on(*units):
        @pl.when(via)
        def _():
            for u in units:
                pltpu.make_async_remote_copy(
                    via_q.at[u], via_q.at[u], via_send.at[0], via_recv.at[u],
                    device_id=(group, via_to), device_id_type=MESH,
                ).wait_recv()
                passed_on(u).start()

    def offer(u, slot):
        for side, there, y in ((0, has_up, ny - 1), (1, has_down, 0)):

            @pl.when(there)
            def _():
                encode(slot, y, hs_q.at[side, u], hs_s.at[side, u])
                post(u, side, hs_q.at[side, u], hs_s.at[side, u])

    def relay(u, x):
        for side, there, y in ((0, has_up, ny - 1), (1, has_down, 0)):
            remote_bytes(x_recv.at[x, y], packet).wait_recv()

            @pl.when(there)
            def _():
                post(u, side, xr_q.at[x, y], xr_s.at[x, y])

    def take_halo(u, slot):
        for side, there, row in ((0, has_down, 0), (1, has_up, ny + 1)):

            @pl.when(there)
            def _():
                remote_bytes(h_recv.at[side, u], packet).wait_recv()
                decode(hr_q.at[side, u], hr_s.at[side, u], slot, row)

            @pl.when(jnp.logical_not(there))
            def _():
                for c in range(4):
                    state[slot, c, row, PAD : PAD + nx, :] = jnp.zeros((nx, nz), F32)

    def take_plane(x, slot, y, wait):
        if wait:
            remote_bytes(x_recv.at[x, y], packet).wait_recv()
        decode(xr_q.at[x, y], xr_s.at[x, y], slot, y + 1)

    lane = lax.broadcasted_iota(jnp.int32, (BLOCK, nz), 1)
    not_first, not_last = lane > 0, lane < nz - 1

    def plane(slot, t, y, target, total):
        for x0 in range(0, nx, BLOCK):
            rows = slice(PAD + x0, PAD + x0 + BLOCK)
            left = slice(PAD + x0 - 1, PAD + x0 + BLOCK - 1)
            right = slice(PAD + x0 + 1, PAD + x0 + BLOCK + 1)
            here = slice(x0, x0 + BLOCK)

            def around(c):
                mid = state[slot, c, y + 1, rows, :]
                below = jnp.where(not_first, pltpu.roll(mid, 1, 1), 0.0)
                above = jnp.where(not_last, pltpu.roll(mid, nz - 1, 1), 0.0)
                return (
                    mid, state[slot, c, y + 1, left, :], state[slot, c, y + 1, right, :],
                    state[slot, c, y, rows, :], state[slot, c, y + 2, rows, :], below, above,
                )

            h, xl, xr, yl, yu, zl, zr = around(3)
            speed = [v_buf[t, c, y, here, :].astype(F32) for c in range(3)]
            turn = speed[0] * (xr - xl) + speed[1] * (yu - yl) + speed[2] * (zr - zl)
            ring = (xl + xr) + (yl + yu) + (zl + zr)
            h_new = 0.28 * h + 0.12 * ring + 0.1 * turn + w_buf[t, y, here, :].astype(F32)
            put(target, 3, y, x0, h_new)
            kh = keep[y, here, :] * h
            a, b = cen[y, here, :], nbr[y, here, :]
            term = None
            for c in range(3):
                m, xl, xr, yl, yu, zl, zr = around(c)
                ring = (xl + xr) + (yl + yu) + (zl + zr)
                new = a * m + b * ring - kh * g_buf[t, c, y, here, :].astype(F32)
                put(target, c, y, x0, new)
                if total is not None:
                    term = speed[c] * new if term is None else term + speed[c] * new
            if total == "set":
                acc[y, here, :] = term
            elif total == "add":
                acc[y, here, :] = acc[y, here, :] + term

    def put(target, c, y, x0, value):
        kind_of, number = target
        if kind_of == "fin":
            fin[number, c, y, x0 : x0 + BLOCK, :] = value
        else:
            state[number, c, y + 1, PAD + x0 : PAD + x0 + BLOCK, :] = value

    def out_copy(t, y):
        return pltpu.make_async_copy(fin.at[t, :, y], out.at[t, :, y], out_sem.at[t])

    def chain(slot, t, target, halo_in=None, halo_out=None, cross_out=None, total=None, crosses=0, passes=()):
        due = [next(order) for _ in range(crosses)]

        def one(i, carry):
            for u, at in passes:

                @pl.when(i == at)
                def _(u=u):
                    pass_on(u)

            if halo_in is None:
                y = lax.rem(i + ny - 1, ny)
            else:
                y = lax.rem(i + 1, ny)

                @pl.when(i == ny - 2)
                def _():
                    take_halo(halo_in, slot)

            plane(slot, t, y, target, total)
            if cross_out is not None:
                encode_crossing(cross_out, target[1], y)
            if target[0] == "fin":
                out_copy(t, y).start()
            if halo_out is not None:

                @pl.when(i == (1 if halo_in is None else ny - 1))
                def _():
                    offer(halo_out, target[1])

            for n, (u, plane_of) in enumerate(due):

                @pl.when(i == 2 + 2 * n)
                def _(u=u, plane_of=plane_of):
                    cross(u, plane_of)

            return carry

        lax.fori_loop(0, ny, one, 0)

    def take_crossing(x, slot):
        def one(i, carry):
            take_plane(x, slot, i, True)
            return carry

        lax.fori_loop(1, ny - 1, one, 0)
        take_plane(x, slot, 0, False)
        take_plane(x, slot, ny - 1, False)

    loaded("state 2")
    load_state(3)
    load_state(1)
    offer(1, 2)
    loaded("state 0")
    load("cells", 4, (density, d_buf), (kind, k_buf), (inlet, i_buf))
    for t in (1, 2, 0, 3):
        load_flow(t)

    def first(i, carry):
        encode_crossing(0, 0, lax.rem(i + ny - 1, ny))

        @pl.when(i == 1)
        def _():
            cross(*next(order))
            cross(*next(order))

        return carry

    lax.fori_loop(0, ny, first, 0)
    for u, t in ((2, 3), (0, 1)):
        loaded(f"state {t}")
        offer(u, t)
    loaded("cells")

    def prepare(y, carry):
        rho = rho_of(d_buf[y], k_buf[y])
        under = 1.0 / (0.5 + rho)
        open_ = (1 - i_buf[y]).astype(F32)
        keep[y] = open_
        nbr[y] = 0.12 * open_
        cen[y] = open_ * (0.28 - 0.25 * (1.0 - rho) * under)
        d_buf[y] = jnp.where(k_buf[y] == 0, -0.375 * under * under, 0.0)
        return carry

    lax.fori_loop(0, ny, prepare, 0)

    def ready(t):
        loaded(f"flow {t}")

    S = "state"
    ready(1)
    chain(2, 1, (S, 5), halo_in=1, halo_out=3, crosses=3, passes=((1, 3), (2, 5), (0, 6)))
    relay(4, 0)
    ready(2)
    take_halo(2, 3)
    chain(3, 2, (S, 2), halo_out=5, crosses=3, passes=((3, 2),))
    ready(0)
    take_halo(0, 1)
    chain(1, 0, (S, 4), cross_out=1, passes=((4, 0), (5, 2)))
    ready(3)
    take_crossing(0, 0)
    take_halo(4, 0)
    chain(0, 3, (S, 1), halo_out=6, crosses=3)
    take_halo(3, 5)
    chain(5, 0, (S, 4), cross_out=2, crosses=3, passes=((6, 2),))
    relay(8, 1)
    take_halo(5, 2)
    chain(2, 1, (S, 3), halo_out=7, crosses=3, passes=((8, 6),))
    take_halo(6, 1)
    chain(1, 2, (S, 5), halo_out=9, crosses=3, passes=((7, 2),))
    take_crossing(1, 0)
    take_halo(8, 0)
    chain(0, 3, (S, 4), halo_out=10, crosses=3, passes=((9, 2),))
    take_halo(7, 3)
    chain(3, 0, ("fin", 0), total="set", crosses=1, passes=((10, 2),))
    relay(11, 2)
    take_halo(9, 5)
    chain(5, 1, ("fin", 1), total="add", passes=((11, 6),))
    take_halo(10, 4)
    chain(4, 2, ("fin", 2), total="add")

    def mine(k):
        return 2 * k + core

    def theirs(k):
        return 2 * k + 1 - core

    def send(n, k, src, dst, other):
        return pltpu.make_async_remote_copy(
            src, dst, s_send.at[0], s_recv.at[n, k], device_id=(other, tile), device_id_type=MESH
        )

    def to_partner(k):
        return send(0, k, acc.at[theirs(k)], near.at[k], partner)

    def to_other_chip(k):
        return send(1, k, half.at[k], far.at[k], across)

    def back(k, y):
        return send(2, k, whole.at[y], whole.at[y], partner)

    def sens_copy(y):
        return pltpu.make_async_copy(whole.at[y], sens.at[y], out_sem.at[4])

    def sum_chip(k):
        to_partner(k).wait_recv()
        half[k] = acc[mine(k)] + near[k]
        to_other_chip(k).start()

    def sum_all(k):
        to_other_chip(k).wait_recv()
        y = mine(k)
        whole[y] = d_buf[y] * (half[k] + far[k])
        back(k, y).start()
        sens_copy(y).start()

    take_halo(11, 0)
    take_plane(2, 0, 0, False)
    take_plane(2, 0, ny - 1, False)

    def last_pair(k, carry):
        @pl.when(k < ny // 2 - 1)
        def _():
            take_plane(2, 0, 2 * k + 1, True)
            take_plane(2, 0, 2 * k + 2, True)

        def one(y, carry):
            plane(0, 3, y, ("fin", 3), "add")
            out_copy(3, y).start()
            return carry

        lax.fori_loop(2 * k, 2 * k + 2, one, 0)
        to_partner(k).start()

        @pl.when(k > 0)
        def _():
            sum_chip(k - 1)

        @pl.when(k > 1)
        def _():
            sum_all(k - 2)

        return carry

    pairs = ny // 2
    lax.fori_loop(0, pairs, last_pair, 0)
    sum_chip(pairs - 1)
    sum_all(pairs - 2)
    sum_all(pairs - 1)
    for k in range(pairs):
        back(k, theirs(k)).wait_recv()
        sens_copy(theirs(k)).start()

    def sent(sem, *refs):
        remote_bytes(sem, tiles_in(*refs)).wait_send()

    sent(s_send.at[0], near, far, half)
    sent(x_send.at[0], xs_q, xs_s)
    for side, there in ((0, has_up), (1, has_down)):

        @pl.when(there)
        def _():
            sent(h_send.at[side], hs_q.at[side], hs_s.at[side])

    @pl.when(via)
    def _():
        sent(via_send.at[0], via_q)

    for t in range(4):
        pltpu.make_async_copy(fin.at[t], out.at[t], out_sem.at[t]).wait()
    pltpu.make_async_copy(whole, sens, out_sem.at[4]).wait()


def hand_over(state, total, state_out, total_out, buf, into, onto):
    phases, ny = state.shape[0], state.shape[2]
    pieces = [(state.at[t, c], state_out.at[t, c]) for t in range(phases) for c in range(4)] + [(total, total_out)]
    ins = [pltpu.make_async_copy(a, buf.at[n], into.at[n]) for n, (a, _) in enumerate(pieces)]
    outs = [pltpu.make_async_copy(buf.at[n], b, onto.at[n]) for n, (_, b) in enumerate(pieces)]
    for copy in ins:
        copy.start()
    for a, b in zip(ins, outs, strict=True):
        a.wait()
        b.start()
    for copy in outs:
        copy.wait()


def on_device(tiles, adjoint_in, velocity, temp_grad, heat_weight, density, cell_kind, inlet):
    phases, _, ny, nx, nz = adjoint_in.shape
    bf16, i16, i32 = jnp.bfloat16, jnp.int16, jnp.int32
    vmem, dma = pltpu.VMEM, pltpu.SemaphoreType.DMA
    shapes = (
        jax.ShapeDtypeStruct(adjoint_in.shape, F32),
        jax.ShapeDtypeStruct(density.shape, F32),
    )
    anywhere = pl.BlockSpec(memory_space=pl.ANY)
    results = pl.pallas_call(
        functools.partial(kernel, tiles),
        out_shape=shapes,
        in_specs=[anywhere] * 7,
        out_specs=[anywhere] * 2,
        scratch_shapes=[
            vmem((6, 4, ny + 2, nx + 2 * PAD, nz), F32),
            vmem((phases, 4, ny, nx, nz), F32),
            vmem((phases, 3, ny, nx, nz), bf16),
            vmem((phases, 3, ny, nx, nz), bf16),
            vmem((phases, ny, nx, nz), bf16),
            vmem((ny, nx, nz), F32),
            vmem((ny, nx, nz), i32),
            vmem((ny, nx, nz), i32),
            vmem((ny, nx, nz), F32),
            vmem((ny, nx, nz), F32),
            vmem((ny, nx, nz), F32),
            vmem((ny, nx, nz), F32),
            vmem((ny // 2, nx, nz), F32),
            vmem((ny // 2, nx, nz), F32),
            vmem((ny // 2, nx, nz), F32),
            vmem((ny, nx, nz), F32),
            vmem((3, ny, 4, nx, nz), i16),
            vmem((3, ny, 8, nz), F32),
            vmem((3, ny, 4, nx, nz), i16),
            vmem((3, ny, 8, nz), F32),
            vmem((2, 12, 4, nx, nz), i16),
            vmem((2, 12, 8, nz), F32),
            vmem((2, 12, 4, nx, nz), i16),
            vmem((2, 12, 8, nz), F32),
            vmem((12, nx, nz), i16),
            vmem((24 * (8 * nx * nz // TILE + 1), TILE // (4 * nz), nz), F32),
            dma((9,)),
            dma((5,)),
            dma((1,)),
            dma((3, ny)),
            dma((2,)),
            dma((2, 12)),
            dma((1,)),
            dma((3, ny // 2)),
            dma((1,)),
            dma((12,)),
        ],
        compiler_params=pltpu.CompilerParams(
            collective_id=0, has_side_effects=True, vmem_limit_bytes=60 * 2**20
        ),
    )(adjoint_in, velocity, temp_grad, heat_weight, density, cell_kind, inlet)
    pieces = 4 * phases + 1
    return pl.pallas_call(
        hand_over,
        out_shape=shapes,
        in_specs=[pl.BlockSpec(memory_space=pltpu.HBM)] * 2,
        out_specs=[anywhere] * 2,
        scratch_shapes=[vmem((pieces, ny, nx, nz), F32), dma((pieces,)), dma((pieces,))],
        compiler_params=pltpu.CompilerParams(vmem_limit_bytes=60 * 2**20),
    )(*results)


def solution(mesh):
    return jax.shard_map(
        functools.partial(on_device, mesh.shape["tile"]),
        mesh=mesh,
        in_specs=(
            P("phase", None, "tile", None, None),
            P("phase", None, "tile", None, None),
            P("phase", None, "tile", None, None),
            P("phase", "tile", None, None),
            P("tile", None, None),
            P("tile", None, None),
            P("tile", None, None),
        ),
        out_specs=(P("phase", None, "tile", None, None), P("tile", None, None)),
        check_vma=False,
    )
```

```python
import functools
import math

import jax
import jax.numpy as jnp
from jax import lax
from jax.experimental import pallas as pl
from jax.experimental.pallas import tpu as pltpu
from jax.sharding import PartitionSpec as P

F32 = jnp.float32
PAD = 8
BLOCK = 32
TOP = 32767.0
TILE = 4096
MESH = pl.DeviceIdType.MESH


def rho_of(density, kind):
    return jnp.where(kind == 0, density, jnp.where(kind == 2, 1.0, 0.0))


def kernel(
    tiles, adj, vel, grad, heat, density, kind, inlet, out, sens,
    state, fin, v_buf, g_buf, w_buf, d_buf, k_buf, i_buf, cen, nbr, keep, acc, half, near, far, whole,
    xs_q, xs_s, xr_q, xr_s, hs_q, hs_s, hr_q, hr_s, via_q, tiles_of,
    load_sem, out_sem, x_send, x_recv, h_send, h_recv, s_send, s_recv, via_send, via_recv,
):
    ny, nx, nz = d_buf.shape
    group, tile = lax.axis_index("phase"), lax.axis_index("tile")
    core = lax.rem(group, 2)
    lower = 1 - tile // (tiles // 2)
    place = lower * tile + (1 - lower) * (tiles - 1 - tile)
    vias = (0, 3, 12)
    via = (place == vias[0]) | (place == vias[1]) | (place == vias[2])
    via_part = 1 + place // 3 - 2 * (place // 12)
    meets = place == tiles // 2 - 1
    lower_end, upper_end = tiles // 2 - 1, tiles // 2
    via_from = lower * lower_end + (1 - lower) * upper_end
    via_to = tiles - 1 - via_from
    before, after, across = (lax.rem(group + n, 4) for n in (3, 1, 2))
    partner = group + 1 - 2 * core
    has_down, has_up = tile > 0, tile < tiles - 1
    body = pl.ds(PAD, nx)

    loads = {}

    def load(name, number, *pairs):
        for src, dst in pairs:
            pltpu.make_async_copy(src, dst, load_sem.at[number]).start()
        loads[name] = (number, tiles_in(*(dst for _, dst in pairs)))

    def tiles_in(*refs):
        return sum(math.prod(r.shape) * jnp.dtype(r.dtype).itemsize for r in refs) // TILE

    def await_local(sem, n):
        pltpu.make_async_copy(tiles_of.at[pl.ds(0, n)], tiles_of.at[pl.ds(0, n)], sem).wait()

    def remote_bytes(sem, n):
        length = tiles_of.at[pl.ds(0, n)]
        return pltpu.make_async_remote_copy(
            length, length, sem, sem, device_id=(before, tile), device_id_type=MESH
        )

    packet = tiles_in(xs_q.at[0, 0], xs_s.at[0, 0])

    def loaded(name):
        number, size = loads[name]
        await_local(load_sem.at[number], size)

    def load_state(t):
        load(f"state {t}", t, (adj.at[t], state.at[t, :, pl.ds(1, ny), body, :]))

    def load_flow(t):
        here = ((vel.at[t], v_buf.at[t]), (grad.at[t], g_buf.at[t]), (heat.at[t], w_buf.at[t]))
        load(f"flow {t}", 5 + t, *here)

    load_state(2)
    load_state(0)

    edge = jnp.zeros((PAD, nz), F32)

    def clear(y, carry):
        for slot in range(state.shape[0]):
            for c in range(4):
                state[slot, c, y, 0:PAD, :] = edge
                state[slot, c, y, PAD + nx : 2 * PAD + nx, :] = edge
        return carry

    lax.fori_loop(0, ny + 2, clear, 0)

    barrier = pltpu.get_barrier_semaphore()
    for other in (before, after, across):
        pl.semaphore_signal(barrier, 1, device_id=(other, tile), device_id_type=MESH)

    @pl.when(has_down)
    def _():
        pl.semaphore_signal(barrier, 1, device_id=(group, tile - 1), device_id_type=MESH)

    @pl.when(has_up)
    def _():
        pl.semaphore_signal(barrier, 1, device_id=(group, tile + 1), device_id_type=MESH)

    @pl.when(via)
    def _():
        pl.semaphore_signal(barrier, 1, device_id=(group, via_from), device_id_type=MESH)

    @pl.when(meets)
    def _():
        for v in vias:
            other = (1 - lower) * v + lower * (tiles - 1 - v)
            pl.semaphore_signal(barrier, 1, device_id=(group, other), device_id_type=MESH)

    extra = via.astype(jnp.int32) + 3 * meets.astype(jnp.int32)
    pl.semaphore_wait(barrier, 3 + has_down.astype(jnp.int32) + has_up.astype(jnp.int32) + extra)

    def encode(slot, y, q, s):
        for c in range(4):
            v = state[slot, c, y + 1, PAD : PAD + nx, :]
            top = jnp.maximum(jnp.max(jnp.abs(v), axis=0, keepdims=True), 1e-30)
            q[c] = jnp.round(v * (TOP / top)).astype(jnp.int32).astype(jnp.int16)
            scale = top * (1.0 / TOP)
            s[c : c + 1, :] = scale
            s[c + 4 : c + 5, :] = scale

    def decode(q, s, slot, row):
        for c in range(4):
            code = q[c].astype(jnp.int32).astype(F32)
            state[slot, c, row, PAD : PAD + nx, :] = code * s[c : c + 1, :]

    def crossing(u, y):
        return [
            pltpu.make_async_remote_copy(
                a.at[u, y], b.at[u, y], x_send.at[0], x_recv.at[u, y],
                device_id=(before, tile), device_id_type=MESH,
            )
            for a, b in ((xs_q, xr_q), (xs_s, xr_s))
        ]

    order = iter([(u, (i + ny - 1) % ny) for u in range(3) for i in range(ny)])

    def cross(u, y):
        for copy in crossing(u, y):
            copy.start()

    def encode_crossing(u, slot, y):
        encode(slot, y, xs_q.at[u, y], xs_s.at[u, y])

    def halo(u, side, q, s):
        other = tile + 1 - 2 * side
        return [
            pltpu.make_async_remote_copy(
                a, b.at[side, u], h_send.at[side], h_recv.at[side, u],
                device_id=(group, other), device_id_type=MESH,
            )
            for a, b in ((q, hr_q), (s, hr_s))
        ]

    def post(u, side, q, s):
        number, scale = halo(u, side, q, s)
        far_apart = tile == (lower_end, upper_end)[side]

        @pl.when(jnp.logical_not(far_apart))
        def _():
            number.start()

        @pl.when(far_apart)
        def _():
            pltpu.make_async_remote_copy(
                q.at[0], hr_q.at[side, u, 0], h_send.at[side], h_recv.at[side, u],
                device_id=(group, tile + 1 - 2 * side), device_id_type=MESH,
            ).start()
            for c, v in enumerate(vias, 1):
                pltpu.make_async_remote_copy(
                    q.at[c], via_q.at[u], h_send.at[side], via_recv.at[u],
                    device_id=(group, (v, tiles - 1 - v)[side]), device_id_type=MESH,
                ).start()

        scale.start()

    def passed_on(u):
        return pltpu.make_async_remote_copy(
            via_q.at[u], hr_q.at[1 - lower, u, via_part], via_send.at[0], h_recv.at[1 - lower, u],
            device_id=(group, via_to), device_id_type=MESH,
        )

    def pass_on(*units):
        @pl.when(via)
        def _():
            for u in units:
                pltpu.make_async_remote_copy(
                    via_q.at[u], via_q.at[u], via_send.at[0], via_recv.at[u],
                    device_id=(group, via_to), device_id_type=MESH,
                ).wait_recv()
                passed_on(u).start()

    def offer(u, slot):
        for side, there, y in ((0, has_up, ny - 1), (1, has_down, 0)):

            @pl.when(there)
            def _():
                encode(slot, y, hs_q.at[side, u], hs_s.at[side, u])
                post(u, side, hs_q.at[side, u], hs_s.at[side, u])

    def relay(u, x):
        for side, there, y in ((0, has_up, ny - 1), (1, has_down, 0)):
            remote_bytes(x_recv.at[x, y], packet).wait_recv()

            @pl.when(there)
            def _():
                post(u, side, xr_q.at[x, y], xr_s.at[x, y])

    def take_halo(u, slot):
        for side, there, row in ((0, has_down, 0), (1, has_up, ny + 1)):

            @pl.when(there)
            def _():
                remote_bytes(h_recv.at[side, u], packet).wait_recv()
                decode(hr_q.at[side, u], hr_s.at[side, u], slot, row)

            @pl.when(jnp.logical_not(there))
            def _():
                for c in range(4):
                    state[slot, c, row, PAD : PAD + nx, :] = jnp.zeros((nx, nz), F32)

    def take_plane(x, slot, y, wait):
        if wait:
            remote_bytes(x_recv.at[x, y], packet).wait_recv()
        decode(xr_q.at[x, y], xr_s.at[x, y], slot, y + 1)

    lane = lax.broadcasted_iota(jnp.int32, (BLOCK, nz), 1)
    not_first, not_last = lane > 0, lane < nz - 1

    def plane(slot, t, y, target, total):
        for x0 in range(0, nx, BLOCK):
            rows = slice(PAD + x0, PAD + x0 + BLOCK)
            left = slice(PAD + x0 - 1, PAD + x0 + BLOCK - 1)
            right = slice(PAD + x0 + 1, PAD + x0 + BLOCK + 1)
            here = slice(x0, x0 + BLOCK)

            def around(c):
                mid = state[slot, c, y + 1, rows, :]
                below = jnp.where(not_first, pltpu.roll(mid, 1, 1), 0.0)
                above = jnp.where(not_last, pltpu.roll(mid, nz - 1, 1), 0.0)
                return (
                    mid, state[slot, c, y + 1, left, :], state[slot, c, y + 1, right, :],
                    state[slot, c, y, rows, :], state[slot, c, y + 2, rows, :], below, above,
                )

            h, xl, xr, yl, yu, zl, zr = around(3)
            speed = [v_buf[t, c, y, here, :].astype(F32) for c in range(3)]
            turn = speed[0] * (xr - xl) + speed[1] * (yu - yl) + speed[2] * (zr - zl)
            ring = (xl + xr) + (yl + yu) + (zl + zr)
            h_new = 0.28 * h + 0.12 * ring + 0.1 * turn + w_buf[t, y, here, :].astype(F32)
            put(target, 3, y, x0, h_new)
            kh = keep[y, here, :] * h
            a, b = cen[y, here, :], nbr[y, here, :]
            term = None
            for c in range(3):
                m, xl, xr, yl, yu, zl, zr = around(c)
                ring = (xl + xr) + (yl + yu) + (zl + zr)
                new = a * m + b * ring - kh * g_buf[t, c, y, here, :].astype(F32)
                put(target, c, y, x0, new)
                if total is not None:
                    term = speed[c] * new if term is None else term + speed[c] * new
            if total == "set":
                acc[y, here, :] = term
            elif total == "add":
                acc[y, here, :] = acc[y, here, :] + term

    def put(target, c, y, x0, value):
        kind_of, number = target
        if kind_of == "fin":
            fin[number, c, y, x0 : x0 + BLOCK, :] = value
        else:
            state[number, c, y + 1, PAD + x0 : PAD + x0 + BLOCK, :] = value

    def out_copy(t, y):
        return pltpu.make_async_copy(fin.at[t, :, y], out.at[t, :, y], out_sem.at[t])

    def chain(slot, t, target, halo_in=None, halo_out=None, cross_out=None, total=None, crosses=0, passes=()):
        due = [next(order) for _ in range(crosses)]

        def one(i, carry):
            for u, at in passes:

                @pl.when(i == at)
                def _(u=u):
                    pass_on(u)

            if halo_in is None:
                y = lax.rem(i + ny - 1, ny)
            else:
                y = lax.rem(i + 1, ny)

                @pl.when(i == ny - 2)
                def _():
                    take_halo(halo_in, slot)

            plane(slot, t, y, target, total)
            if cross_out is not None:
                encode_crossing(cross_out, target[1], y)
            if target[0] == "fin":
                out_copy(t, y).start()
            if halo_out is not None:

                @pl.when(i == (1 if halo_in is None else ny - 1))
                def _():
                    offer(halo_out, target[1])

            for n, (u, plane_of) in enumerate(due):

                @pl.when(i == (3, 6)[n])
                def _(u=u, plane_of=plane_of):
                    cross(u, plane_of)

            return carry

        lax.fori_loop(0, ny, one, 0)

    def take_crossing(x, slot):
        def one(i, carry):
            take_plane(x, slot, i, True)
            return carry

        lax.fori_loop(1, ny - 1, one, 0)
        take_plane(x, slot, 0, False)
        take_plane(x, slot, ny - 1, False)

    loaded("state 2")
    load_state(3)
    load_state(1)
    offer(1, 2)
    loaded("state 0")
    load("cells", 4, (density, d_buf), (kind, k_buf), (inlet, i_buf))
    for t in (1, 2, 0, 3):
        load_flow(t)

    def first(i, carry):
        encode_crossing(0, 0, lax.rem(i + ny - 1, ny))

        @pl.when(i == 1)
        def _():
            cross(*next(order))
            cross(*next(order))

        return carry

    lax.fori_loop(0, ny, first, 0)
    for u, t in ((2, 3), (0, 1)):
        loaded(f"state {t}")
        offer(u, t)
    loaded("cells")

    def prepare(y, carry):
        rho = rho_of(d_buf[y], k_buf[y])
        under = 1.0 / (0.5 + rho)
        open_ = (1 - i_buf[y]).astype(F32)
        keep[y] = open_
        nbr[y] = 0.12 * open_
        cen[y] = open_ * (0.28 - 0.25 * (1.0 - rho) * under)
        d_buf[y] = jnp.where(k_buf[y] == 0, -0.375 * under * under, 0.0)
        return carry

    lax.fori_loop(0, ny, prepare, 0)

    def ready(t):
        loaded(f"flow {t}")

    S = "state"
    ready(1)
    chain(2, 1, (S, 5), halo_in=1, halo_out=3, passes=((1, 3), (2, 5), (0, 6)), crosses=2)
    relay(4, 0)
    ready(2)
    take_halo(2, 3)
    chain(3, 2, (S, 2), halo_out=5, passes=((3, 5),), crosses=2)
    ready(0)
    take_halo(0, 1)
    chain(1, 0, (S, 4), cross_out=1, passes=((4, 0), (5, 5)), crosses=2)
    ready(3)
    take_crossing(0, 0)
    take_halo(4, 0)
    chain(0, 3, (S, 1), halo_out=6, crosses=2)
    take_halo(3, 5)
    chain(5, 0, (S, 4), cross_out=2, passes=((6, 5),), crosses=2)
    relay(8, 1)
    take_halo(5, 2)
    chain(2, 1, (S, 3), halo_out=7, passes=((8, 6),), crosses=2)
    take_halo(6, 1)
    chain(1, 2, (S, 5), halo_out=9, passes=((7, 5),), crosses=2)
    take_crossing(1, 0)
    take_halo(8, 0)
    chain(0, 3, (S, 4), halo_out=10, passes=((9, 5),), crosses=2)
    take_halo(7, 3)
    chain(3, 0, ("fin", 0), total="set", passes=((10, 5),), crosses=2)
    relay(11, 2)
    take_halo(9, 5)
    chain(5, 1, ("fin", 1), total="add", passes=((11, 6),), crosses=2)
    take_halo(10, 4)
    chain(4, 2, ("fin", 2), total="add", crosses=2)

    def mine(k):
        return 2 * k + core

    def theirs(k):
        return 2 * k + 1 - core

    def send(n, k, src, dst, other):
        return pltpu.make_async_remote_copy(
            src, dst, s_send.at[0], s_recv.at[n, k], device_id=(other, tile), device_id_type=MESH
        )

    def to_partner(k):
        return send(0, k, acc.at[theirs(k)], near.at[k], partner)

    def to_other_chip(k):
        return send(1, k, half.at[k], far.at[k], across)

    def back(k, y):
        return send(2, k, whole.at[y], whole.at[y], partner)

    def sens_copy(y):
        return pltpu.make_async_copy(whole.at[y], sens.at[y], out_sem.at[4])

    def sum_chip(k):
        to_partner(k).wait_recv()
        half[k] = acc[mine(k)] + near[k]
        to_other_chip(k).start()

    def sum_all(k):
        to_other_chip(k).wait_recv()
        y = mine(k)
        whole[y] = d_buf[y] * (half[k] + far[k])
        back(k, y).start()
        sens_copy(y).start()

    take_halo(11, 0)
    take_plane(2, 0, 0, False)
    take_plane(2, 0, ny - 1, False)

    def last_pair(k, carry):
        @pl.when(k < ny // 2 - 1)
        def _():
            take_plane(2, 0, 2 * k + 1, True)
            take_plane(2, 0, 2 * k + 2, True)

        def one(y, carry):
            plane(0, 3, y, ("fin", 3), "add")
            out_copy(3, y).start()
            return carry

        lax.fori_loop(2 * k, 2 * k + 2, one, 0)
        to_partner(k).start()

        @pl.when(k > 0)
        def _():
            sum_chip(k - 1)

        @pl.when(k > 1)
        def _():
            sum_all(k - 2)

        return carry

    pairs = ny // 2
    lax.fori_loop(0, pairs, last_pair, 0)
    sum_chip(pairs - 1)
    sum_all(pairs - 2)
    sum_all(pairs - 1)
    for k in range(pairs):
        back(k, theirs(k)).wait_recv()
        sens_copy(theirs(k)).start()

    def sent(sem, *refs):
        remote_bytes(sem, tiles_in(*refs)).wait_send()

    sent(s_send.at[0], near, far, half)
    sent(x_send.at[0], xs_q, xs_s)
    for side, there in ((0, has_up), (1, has_down)):

        @pl.when(there)
        def _():
            sent(h_send.at[side], hs_q.at[side], hs_s.at[side])

    @pl.when(via)
    def _():
        sent(via_send.at[0], via_q)

    for t in range(4):
        pltpu.make_async_copy(fin.at[t], out.at[t], out_sem.at[t]).wait()
    pltpu.make_async_copy(whole, sens, out_sem.at[4]).wait()


def hand_over(state, total, state_out, total_out, buf, into, onto):
    phases, ny = state.shape[0], state.shape[2]
    pieces = [(state.at[t, c], state_out.at[t, c]) for t in range(phases) for c in range(4)] + [(total, total_out)]
    ins = [pltpu.make_async_copy(a, buf.at[n], into.at[n]) for n, (a, _) in enumerate(pieces)]
    outs = [pltpu.make_async_copy(buf.at[n], b, onto.at[n]) for n, (_, b) in enumerate(pieces)]
    for copy in ins:
        copy.start()
    for a, b in zip(ins, outs, strict=True):
        a.wait()
        b.start()
    for copy in outs:
        copy.wait()


def on_device(tiles, adjoint_in, velocity, temp_grad, heat_weight, density, cell_kind, inlet):
    phases, _, ny, nx, nz = adjoint_in.shape
    bf16, i16, i32 = jnp.bfloat16, jnp.int16, jnp.int32
    vmem, dma = pltpu.VMEM, pltpu.SemaphoreType.DMA
    shapes = (
        jax.ShapeDtypeStruct(adjoint_in.shape, F32),
        jax.ShapeDtypeStruct(density.shape, F32),
    )
    anywhere = pl.BlockSpec(memory_space=pl.ANY)
    results = pl.pallas_call(
        functools.partial(kernel, tiles),
        out_shape=shapes,
        in_specs=[anywhere] * 7,
        out_specs=[anywhere] * 2,
        scratch_shapes=[
            vmem((6, 4, ny + 2, nx + 2 * PAD, nz), F32),
            vmem((phases, 4, ny, nx, nz), F32),
            vmem((phases, 3, ny, nx, nz), bf16),
            vmem((phases, 3, ny, nx, nz), bf16),
            vmem((phases, ny, nx, nz), bf16),
            vmem((ny, nx, nz), F32),
            vmem((ny, nx, nz), i32),
            vmem((ny, nx, nz), i32),
            vmem((ny, nx, nz), F32),
            vmem((ny, nx, nz), F32),
            vmem((ny, nx, nz), F32),
            vmem((ny, nx, nz), F32),
            vmem((ny // 2, nx, nz), F32),
            vmem((ny // 2, nx, nz), F32),
            vmem((ny // 2, nx, nz), F32),
            vmem((ny, nx, nz), F32),
            vmem((3, ny, 4, nx, nz), i16),
            vmem((3, ny, 8, nz), F32),
            vmem((3, ny, 4, nx, nz), i16),
            vmem((3, ny, 8, nz), F32),
            vmem((2, 12, 4, nx, nz), i16),
            vmem((2, 12, 8, nz), F32),
            vmem((2, 12, 4, nx, nz), i16),
            vmem((2, 12, 8, nz), F32),
            vmem((12, nx, nz), i16),
            vmem((24 * (8 * nx * nz // TILE + 1), TILE // (4 * nz), nz), F32),
            dma((9,)),
            dma((5,)),
            dma((1,)),
            dma((3, ny)),
            dma((2,)),
            dma((2, 12)),
            dma((1,)),
            dma((3, ny // 2)),
            dma((1,)),
            dma((12,)),
        ],
        compiler_params=pltpu.CompilerParams(
            collective_id=0, has_side_effects=True, vmem_limit_bytes=60 * 2**20
        ),
    )(adjoint_in, velocity, temp_grad, heat_weight, density, cell_kind, inlet)
    pieces = 4 * phases + 1
    return pl.pallas_call(
        hand_over,
        out_shape=shapes,
        in_specs=[pl.BlockSpec(memory_space=pltpu.HBM)] * 2,
        out_specs=[anywhere] * 2,
        scratch_shapes=[vmem((pieces, ny, nx, nz), F32), dma((pieces,)), dma((pieces,))],
        compiler_params=pltpu.CompilerParams(vmem_limit_bytes=60 * 2**20),
    )(*results)


def solution(mesh):
    return jax.shard_map(
        functools.partial(on_device, mesh.shape["tile"]),
        mesh=mesh,
        in_specs=(
            P("phase", None, "tile", None, None),
            P("phase", None, "tile", None, None),
            P("phase", None, "tile", None, None),
            P("phase", "tile", None, None),
            P("tile", None, None),
            P("tile", None, None),
            P("tile", None, None),
        ),
        out_specs=(P("phase", None, "tile", None, None), P("tile", None, None)),
        check_vma=False,
    )
```

```python
import functools
import math

import jax
import jax.numpy as jnp
from jax import lax
from jax.experimental import pallas as pl
from jax.experimental.pallas import tpu as pltpu
from jax.sharding import PartitionSpec as P

F32 = jnp.float32
PAD = 8
BLOCK = 32
TOP = 32767.0
TILE = 4096
MESH = pl.DeviceIdType.MESH


def rho_of(density, kind):
    return jnp.where(kind == 0, density, jnp.where(kind == 2, 1.0, 0.0))


def kernel(
    tiles, adj, vel, grad, heat, density, kind, inlet, out, sens,
    state, fin, v_buf, g_buf, w_buf, d_buf, k_buf, i_buf, cen, nbr, keep, acc, half, near, far, whole,
    xs_q, xs_s, xr_q, xr_s, hs_q, hs_s, hr_q, hr_s, via_q, tiles_of,
    load_sem, out_sem, x_send, x_recv, h_send, h_recv, s_send, s_recv, via_send, via_recv,
):
    ny, nx, nz = d_buf.shape
    group, tile = lax.axis_index("phase"), lax.axis_index("tile")
    core = lax.rem(group, 2)
    lower = 1 - tile // (tiles // 2)
    place = lower * tile + (1 - lower) * (tiles - 1 - tile)
    vias = (0, 3, 12)
    via = (place == vias[0]) | (place == vias[1]) | (place == vias[2])
    via_part = 1 + place // 3 - 2 * (place // 12)
    meets = place == tiles // 2 - 1
    lower_end, upper_end = tiles // 2 - 1, tiles // 2
    via_from = lower * lower_end + (1 - lower) * upper_end
    via_to = tiles - 1 - via_from
    before, after, across = (lax.rem(group + n, 4) for n in (3, 1, 2))
    partner = group + 1 - 2 * core
    has_down, has_up = tile > 0, tile < tiles - 1
    body = pl.ds(PAD, nx)

    loads = {}

    def load(name, number, *pairs):
        for src, dst in pairs:
            pltpu.make_async_copy(src, dst, load_sem.at[number]).start()
        loads[name] = (number, tiles_in(*(dst for _, dst in pairs)))

    def tiles_in(*refs):
        return sum(math.prod(r.shape) * jnp.dtype(r.dtype).itemsize for r in refs) // TILE

    def await_local(sem, n):
        pltpu.make_async_copy(tiles_of.at[pl.ds(0, n)], tiles_of.at[pl.ds(0, n)], sem).wait()

    def remote_bytes(sem, n):
        length = tiles_of.at[pl.ds(0, n)]
        return pltpu.make_async_remote_copy(
            length, length, sem, sem, device_id=(before, tile), device_id_type=MESH
        )

    packet = tiles_in(xs_q.at[0, 0], xs_s.at[0, 0])

    def loaded(name):
        number, size = loads[name]
        await_local(load_sem.at[number], size)

    def load_state(t):
        load(f"state {t}", t, (adj.at[t], state.at[t, :, pl.ds(1, ny), body, :]))

    def load_flow(t):
        here = ((vel.at[t], v_buf.at[t]), (grad.at[t], g_buf.at[t]), (heat.at[t], w_buf.at[t]))
        load(f"flow {t}", 5 + t, *here)

    load_state(2)
    load_state(0)

    edge = jnp.zeros((PAD, nz), F32)

    def clear(y, carry):
        for slot in range(state.shape[0]):
            for c in range(4):
                state[slot, c, y, 0:PAD, :] = edge
                state[slot, c, y, PAD + nx : 2 * PAD + nx, :] = edge
        return carry

    lax.fori_loop(0, ny + 2, clear, 0)

    barrier = pltpu.get_barrier_semaphore()
    for other in (before, after, across):
        pl.semaphore_signal(barrier, 1, device_id=(other, tile), device_id_type=MESH)

    @pl.when(has_down)
    def _():
        pl.semaphore_signal(barrier, 1, device_id=(group, tile - 1), device_id_type=MESH)

    @pl.when(has_up)
    def _():
        pl.semaphore_signal(barrier, 1, device_id=(group, tile + 1), device_id_type=MESH)

    @pl.when(via)
    def _():
        pl.semaphore_signal(barrier, 1, device_id=(group, via_from), device_id_type=MESH)

    @pl.when(meets)
    def _():
        for v in vias:
            other = (1 - lower) * v + lower * (tiles - 1 - v)
            pl.semaphore_signal(barrier, 1, device_id=(group, other), device_id_type=MESH)

    extra = via.astype(jnp.int32) + 3 * meets.astype(jnp.int32)
    pl.semaphore_wait(barrier, 3 + has_down.astype(jnp.int32) + has_up.astype(jnp.int32) + extra)

    def encode(slot, y, q, s):
        for c in range(4):
            v = state[slot, c, y + 1, PAD : PAD + nx, :]
            top = jnp.maximum(jnp.max(jnp.abs(v), axis=0, keepdims=True), 1e-30)
            q[c] = jnp.round(v * (TOP / top)).astype(jnp.int32).astype(jnp.int16)
            scale = top * (1.0 / TOP)
            s[c : c + 1, :] = scale
            s[c + 4 : c + 5, :] = scale

    def decode(q, s, slot, row):
        for c in range(4):
            code = q[c].astype(jnp.int32).astype(F32)
            state[slot, c, row, PAD : PAD + nx, :] = code * s[c : c + 1, :]

    def crossing(u, y):
        return [
            pltpu.make_async_remote_copy(
                a.at[u, y], b.at[u, y], x_send.at[0], x_recv.at[u, y],
                device_id=(before, tile), device_id_type=MESH,
            )
            for a, b in ((xs_q, xr_q), (xs_s, xr_s))
        ]

    order = iter([(u, (i + ny - 1) % ny) for u in range(3) for i in range(ny)])

    def cross(u, y):
        for copy in crossing(u, y):
            copy.start()

    def encode_crossing(u, slot, y):
        encode(slot, y, xs_q.at[u, y], xs_s.at[u, y])

    def halo(u, side, q, s):
        other = tile + 1 - 2 * side
        return [
            pltpu.make_async_remote_copy(
                a, b.at[side, u], h_send.at[side], h_recv.at[side, u],
                device_id=(group, other), device_id_type=MESH,
            )
            for a, b in ((q, hr_q), (s, hr_s))
        ]

    def post(u, side, q, s):
        number, scale = halo(u, side, q, s)
        far_apart = tile == (lower_end, upper_end)[side]

        @pl.when(jnp.logical_not(far_apart))
        def _():
            number.start()

        @pl.when(far_apart)
        def _():
            pltpu.make_async_remote_copy(
                q.at[0], hr_q.at[side, u, 0], h_send.at[side], h_recv.at[side, u],
                device_id=(group, tile + 1 - 2 * side), device_id_type=MESH,
            ).start()
            for c, v in enumerate(vias, 1):
                pltpu.make_async_remote_copy(
                    q.at[c], via_q.at[u], h_send.at[side], via_recv.at[u],
                    device_id=(group, (v, tiles - 1 - v)[side]), device_id_type=MESH,
                ).start()

        scale.start()

    def passed_on(u):
        return pltpu.make_async_remote_copy(
            via_q.at[u], hr_q.at[1 - lower, u, via_part], via_send.at[0], h_recv.at[1 - lower, u],
            device_id=(group, via_to), device_id_type=MESH,
        )

    def pass_on(*units):
        @pl.when(via)
        def _():
            for u in units:
                pltpu.make_async_remote_copy(
                    via_q.at[u], via_q.at[u], via_send.at[0], via_recv.at[u],
                    device_id=(group, via_to), device_id_type=MESH,
                ).wait_recv()
                passed_on(u).start()

    def offer(u, slot):
        for side, there, y in ((0, has_up, ny - 1), (1, has_down, 0)):

            @pl.when(there)
            def _():
                encode(slot, y, hs_q.at[side, u], hs_s.at[side, u])
                post(u, side, hs_q.at[side, u], hs_s.at[side, u])

    def relay(u, x):
        for side, there, y in ((0, has_up, ny - 1), (1, has_down, 0)):
            remote_bytes(x_recv.at[x, y], packet).wait_recv()

            @pl.when(there)
            def _():
                post(u, side, xr_q.at[x, y], xr_s.at[x, y])

    def take_halo(u, slot):
        for side, there, row in ((0, has_down, 0), (1, has_up, ny + 1)):

            @pl.when(there)
            def _():
                remote_bytes(h_recv.at[side, u], packet).wait_recv()
                decode(hr_q.at[side, u], hr_s.at[side, u], slot, row)

            @pl.when(jnp.logical_not(there))
            def _():
                for c in range(4):
                    state[slot, c, row, PAD : PAD + nx, :] = jnp.zeros((nx, nz), F32)

    def take_plane(x, slot, y, wait):
        if wait:
            remote_bytes(x_recv.at[x, y], packet).wait_recv()
        decode(xr_q.at[x, y], xr_s.at[x, y], slot, y + 1)

    lane = lax.broadcasted_iota(jnp.int32, (BLOCK, nz), 1)
    not_first, not_last = lane > 0, lane < nz - 1

    def plane(slot, t, y, target, total):
        for x0 in range(0, nx, BLOCK):
            rows = slice(PAD + x0, PAD + x0 + BLOCK)
            left = slice(PAD + x0 - 1, PAD + x0 + BLOCK - 1)
            right = slice(PAD + x0 + 1, PAD + x0 + BLOCK + 1)
            here = slice(x0, x0 + BLOCK)

            def around(c):
                mid = state[slot, c, y + 1, rows, :]
                below = jnp.where(not_first, pltpu.roll(mid, 1, 1), 0.0)
                above = jnp.where(not_last, pltpu.roll(mid, nz - 1, 1), 0.0)
                return (
                    mid, state[slot, c, y + 1, left, :], state[slot, c, y + 1, right, :],
                    state[slot, c, y, rows, :], state[slot, c, y + 2, rows, :], below, above,
                )

            h, xl, xr, yl, yu, zl, zr = around(3)
            speed = [v_buf[t, c, y, here, :].astype(F32) for c in range(3)]
            turn = speed[0] * (xr - xl) + speed[1] * (yu - yl) + speed[2] * (zr - zl)
            ring = (xl + xr) + (yl + yu) + (zl + zr)
            h_new = 0.28 * h + 0.12 * ring + 0.1 * turn + w_buf[t, y, here, :].astype(F32)
            put(target, 3, y, x0, h_new)
            kh = keep[y, here, :] * h
            a, b = cen[y, here, :], nbr[y, here, :]
            term = None
            for c in range(3):
                m, xl, xr, yl, yu, zl, zr = around(c)
                ring = (xl + xr) + (yl + yu) + (zl + zr)
                new = a * m + b * ring - kh * g_buf[t, c, y, here, :].astype(F32)
                put(target, c, y, x0, new)
                if total is not None:
                    term = speed[c] * new if term is None else term + speed[c] * new
            if total == "set":
                acc[y, here, :] = term
            elif total == "add":
                acc[y, here, :] = acc[y, here, :] + term

    def put(target, c, y, x0, value):
        kind_of, number = target
        if kind_of == "fin":
            fin[number % 2, c, y, x0 : x0 + BLOCK, :] = value
        else:
            state[number, c, y + 1, PAD + x0 : PAD + x0 + BLOCK, :] = value

    def out_copy(t, y):
        return pltpu.make_async_copy(fin.at[t % 2, :, y], out.at[t, :, y], out_sem.at[t])

    def chain(slot, t, target, halo_in=None, halo_out=None, cross_out=None, total=None, crosses=0, passes=()):
        due = [next(order) for _ in range(crosses)]

        def one(i, carry):
            for u, at in passes:

                @pl.when(i == at)
                def _(u=u):
                    pass_on(u)

            if halo_in is None:
                y = lax.rem(i + ny - 1, ny)
            else:
                y = lax.rem(i + 1, ny)

                @pl.when(i == ny - 2)
                def _():
                    take_halo(halo_in, slot)

            plane(slot, t, y, target, total)
            if cross_out is not None:
                encode_crossing(cross_out, target[1], y)
            if target[0] == "fin":
                out_copy(t, y).start()
            if halo_out is not None:

                @pl.when(i == (1 if halo_in is None else ny - 1))
                def _():
                    offer(halo_out, target[1])

            for n, (u, plane_of) in enumerate(due):

                @pl.when(i == (3, 6)[n])
                def _(u=u, plane_of=plane_of):
                    cross(u, plane_of)

            return carry

        lax.fori_loop(0, ny, one, 0)

    def written(t):
        pltpu.make_async_copy(fin.at[t % 2], out.at[t], out_sem.at[t]).wait()

    def take_crossing(x, slot):
        def one(i, carry):
            take_plane(x, slot, i, True)
            return carry

        lax.fori_loop(1, ny - 1, one, 0)
        take_plane(x, slot, 0, False)
        take_plane(x, slot, ny - 1, False)

    loaded("state 2")
    load_state(3)
    load_state(1)
    offer(1, 2)
    loaded("state 0")
    load("cells", 4, (density, d_buf), (kind, k_buf), (inlet, i_buf))
    for t in (1, 2, 0, 3):
        load_flow(t)

    def first(i, carry):
        encode_crossing(0, 0, lax.rem(i + ny - 1, ny))

        @pl.when(i == 1)
        def _():
            cross(*next(order))
            cross(*next(order))

        return carry

    lax.fori_loop(0, ny, first, 0)
    for u, t in ((2, 3), (0, 1)):
        loaded(f"state {t}")
        offer(u, t)
    loaded("cells")

    def prepare(y, carry):
        rho = rho_of(d_buf[y], k_buf[y])
        under = 1.0 / (0.5 + rho)
        open_ = (1 - i_buf[y]).astype(F32)
        keep[y] = open_
        nbr[y] = 0.12 * open_
        cen[y] = open_ * (0.28 - 0.25 * (1.0 - rho) * under)
        d_buf[y] = jnp.where(k_buf[y] == 0, -0.375 * under * under, 0.0)
        return carry

    lax.fori_loop(0, ny, prepare, 0)

    def ready(t):
        loaded(f"flow {t}")

    S = "state"
    ready(1)
    chain(2, 1, (S, 5), halo_in=1, halo_out=3, passes=((1, 3), (2, 5), (0, 6)), crosses=2)
    relay(4, 0)
    ready(2)
    take_halo(2, 3)
    chain(3, 2, (S, 2), halo_out=5, passes=((3, 5),), crosses=2)
    ready(0)
    take_halo(0, 1)
    chain(1, 0, (S, 4), cross_out=1, passes=((4, 0), (5, 5)), crosses=2)
    ready(3)
    take_crossing(0, 0)
    take_halo(4, 0)
    chain(0, 3, (S, 1), halo_out=6, crosses=2)
    take_halo(3, 5)
    chain(5, 0, (S, 4), cross_out=2, passes=((6, 5),), crosses=2)
    relay(8, 1)
    take_halo(5, 2)
    chain(2, 1, (S, 3), halo_out=7, passes=((8, 6),), crosses=2)
    take_halo(6, 1)
    chain(1, 2, (S, 5), halo_out=9, passes=((7, 5),), crosses=2)
    take_crossing(1, 0)
    take_halo(8, 0)
    chain(0, 3, (S, 4), halo_out=10, passes=((9, 5),), crosses=2)
    take_halo(7, 3)
    chain(3, 0, ("fin", 0), total="set", passes=((10, 5),), crosses=2)
    relay(11, 2)
    take_halo(9, 5)
    chain(5, 1, ("fin", 1), total="add", passes=((11, 6),), crosses=2)
    written(0)
    take_halo(10, 4)
    chain(4, 2, ("fin", 2), total="add", crosses=2)

    def mine(k):
        return 2 * k + core

    def theirs(k):
        return 2 * k + 1 - core

    def send(n, k, src, dst, other):
        return pltpu.make_async_remote_copy(
            src, dst, s_send.at[0], s_recv.at[n, k], device_id=(other, tile), device_id_type=MESH
        )

    def to_partner(k):
        return send(0, k, acc.at[theirs(k)], near.at[k], partner)

    def to_other_chip(k):
        return send(1, k, half.at[k], far.at[k], across)

    def back(k, y):
        return send(2, k, whole.at[y], whole.at[y], partner)

    def sens_copy(y):
        return pltpu.make_async_copy(whole.at[y], sens.at[y], out_sem.at[4])

    def sum_chip(k):
        to_partner(k).wait_recv()
        half[k] = acc[mine(k)] + near[k]
        to_other_chip(k).start()

    def sum_all(k):
        to_other_chip(k).wait_recv()
        y = mine(k)
        whole[y] = d_buf[y] * (half[k] + far[k])
        back(k, y).start()
        sens_copy(y).start()

    written(1)
    take_halo(11, 0)
    take_plane(2, 0, 0, False)
    take_plane(2, 0, ny - 1, False)

    def last_pair(k, carry):
        @pl.when(k < ny // 2 - 1)
        def _():
            take_plane(2, 0, 2 * k + 1, True)
            take_plane(2, 0, 2 * k + 2, True)

        def one(y, carry):
            plane(0, 3, y, ("fin", 3), "add")
            out_copy(3, y).start()
            return carry

        lax.fori_loop(2 * k, 2 * k + 2, one, 0)
        to_partner(k).start()

        @pl.when(k > 0)
        def _():
            sum_chip(k - 1)

        @pl.when(k > 1)
        def _():
            sum_all(k - 2)

        return carry

    pairs = ny // 2
    lax.fori_loop(0, pairs, last_pair, 0)
    sum_chip(pairs - 1)
    sum_all(pairs - 2)
    sum_all(pairs - 1)
    for k in range(pairs):
        back(k, theirs(k)).wait_recv()
        sens_copy(theirs(k)).start()

    def sent(sem, *refs):
        remote_bytes(sem, tiles_in(*refs)).wait_send()

    sent(s_send.at[0], near, far, half)
    sent(x_send.at[0], xs_q, xs_s)
    for side, there in ((0, has_up), (1, has_down)):

        @pl.when(there)
        def _():
            sent(h_send.at[side], hs_q.at[side], hs_s.at[side])

    @pl.when(via)
    def _():
        sent(via_send.at[0], via_q)

    written(2)
    written(3)
    pltpu.make_async_copy(whole, sens, out_sem.at[4]).wait()


def hand_over(state, total, state_out, total_out, sems):
    phases = state.shape[0]
    copies = [pltpu.make_async_copy(state.at[t], state_out.at[t], sems.at[t]) for t in range(phases)]
    copies.append(pltpu.make_async_copy(total, total_out, sems.at[phases]))
    for copy in copies:
        copy.start()
    for copy in copies:
        copy.wait()


def on_device(tiles, adjoint_in, velocity, temp_grad, heat_weight, density, cell_kind, inlet):
    phases, _, ny, nx, nz = adjoint_in.shape
    bf16, i16, i32 = jnp.bfloat16, jnp.int16, jnp.int32
    vmem, dma = pltpu.VMEM, pltpu.SemaphoreType.DMA
    shapes = (
        jax.ShapeDtypeStruct(adjoint_in.shape, F32),
        jax.ShapeDtypeStruct(density.shape, F32),
    )
    anywhere = pl.BlockSpec(memory_space=pl.ANY)
    results = pl.pallas_call(
        functools.partial(kernel, tiles),
        out_shape=shapes,
        in_specs=[anywhere] * 7,
        out_specs=[anywhere] * 2,
        scratch_shapes=[
            vmem((6, 4, ny + 2, nx + 2 * PAD, nz), F32),
            vmem((2, 4, ny, nx, nz), F32),
            vmem((phases, 3, ny, nx, nz), bf16),
            vmem((phases, 3, ny, nx, nz), bf16),
            vmem((phases, ny, nx, nz), bf16),
            vmem((ny, nx, nz), F32),
            vmem((ny, nx, nz), i32),
            vmem((ny, nx, nz), i32),
            vmem((ny, nx, nz), F32),
            vmem((ny, nx, nz), F32),
            vmem((ny, nx, nz), F32),
            vmem((ny, nx, nz), F32),
            vmem((ny // 2, nx, nz), F32),
            vmem((ny // 2, nx, nz), F32),
            vmem((ny // 2, nx, nz), F32),
            vmem((ny, nx, nz), F32),
            vmem((3, ny, 4, nx, nz), i16),
            vmem((3, ny, 8, nz), F32),
            vmem((3, ny, 4, nx, nz), i16),
            vmem((3, ny, 8, nz), F32),
            vmem((2, 12, 4, nx, nz), i16),
            vmem((2, 12, 8, nz), F32),
            vmem((2, 12, 4, nx, nz), i16),
            vmem((2, 12, 8, nz), F32),
            vmem((12, nx, nz), i16),
            vmem((24 * (8 * nx * nz // TILE + 1), TILE // (4 * nz), nz), F32),
            dma((9,)),
            dma((5,)),
            dma((1,)),
            dma((3, ny)),
            dma((2,)),
            dma((2, 12)),
            dma((1,)),
            dma((3, ny // 2)),
            dma((1,)),
            dma((12,)),
        ],
        compiler_params=pltpu.CompilerParams(
            collective_id=0, has_side_effects=True, vmem_limit_bytes=53 * 2**20
        ),
    )(adjoint_in, velocity, temp_grad, heat_weight, density, cell_kind, inlet)
    return pl.pallas_call(
        hand_over,
        out_shape=shapes,
        in_specs=[anywhere] * 2,
        out_specs=[anywhere] * 2,
        scratch_shapes=[dma((phases + 1,))],
        compiler_params=pltpu.CompilerParams(vmem_limit_bytes=4 * 2**20),
    )(*results)


def solution(mesh):
    return jax.shard_map(
        functools.partial(on_device, mesh.shape["tile"]),
        mesh=mesh,
        in_specs=(
            P("phase", None, "tile", None, None),
            P("phase", None, "tile", None, None),
            P("phase", None, "tile", None, None),
            P("phase", "tile", None, None),
            P("tile", None, None),
            P("tile", None, None),
            P("tile", None, None),
        ),
        out_specs=(P("phase", None, "tile", None, None), P("tile", None, None)),
        check_vma=False,
    )
```

```python
import functools
import math

import jax
import jax.numpy as jnp
from jax import lax
from jax.experimental import pallas as pl
from jax.experimental.pallas import tpu as pltpu
from jax.sharding import PartitionSpec as P

F32 = jnp.float32
PAD = 8
BLOCK = 32
TOP = 32767.0
TILE = 4096
MESH = pl.DeviceIdType.MESH


def rho_of(density, kind):
    return jnp.where(kind == 0, density, jnp.where(kind == 2, 1.0, 0.0))


def kernel(
    tiles, adj, vel, grad, heat, density, kind, inlet, out, sens,
    state, fin, v_buf, g_buf, w_buf, d_buf, k_buf, i_buf, cen, nbr, keep, acc, half, near, far, whole,
    xs_q, xs_s, xr_q, xr_s, hs_q, hs_s, hr_q, hr_s, via_q, tiles_of,
    load_sem, out_sem, x_send, x_recv, h_send, h_recv, s_send, s_recv, via_send, via_recv,
):
    ny, nx, nz = d_buf.shape
    group, tile = lax.axis_index("phase"), lax.axis_index("tile")
    core = lax.rem(group, 2)
    lower = 1 - tile // (tiles // 2)
    place = lower * tile + (1 - lower) * (tiles - 1 - tile)
    vias = (0, 3, 12)
    via = (place == vias[0]) | (place == vias[1]) | (place == vias[2])
    via_part = 1 + place // 3 - 2 * (place // 12)
    meets = place == tiles // 2 - 1
    lower_end, upper_end = tiles // 2 - 1, tiles // 2
    via_from = lower * lower_end + (1 - lower) * upper_end
    via_to = tiles - 1 - via_from
    before, after, across = (lax.rem(group + n, 4) for n in (3, 1, 2))
    partner = group + 1 - 2 * core
    has_down, has_up = tile > 0, tile < tiles - 1
    body = pl.ds(PAD, nx)

    loads = {}

    def load(name, number, *pairs):
        for src, dst in pairs:
            pltpu.make_async_copy(src, dst, load_sem.at[number]).start()
        loads[name] = (number, tiles_in(*(dst for _, dst in pairs)))

    def tiles_in(*refs):
        return sum(math.prod(r.shape) * jnp.dtype(r.dtype).itemsize for r in refs) // TILE

    def await_local(sem, n):
        pltpu.make_async_copy(tiles_of.at[pl.ds(0, n)], tiles_of.at[pl.ds(0, n)], sem).wait()

    def remote_bytes(sem, n):
        length = tiles_of.at[pl.ds(0, n)]
        return pltpu.make_async_remote_copy(
            length, length, sem, sem, device_id=(before, tile), device_id_type=MESH
        )

    packet = tiles_in(xs_q.at[0, 0], xs_s.at[0, 0])

    def loaded(name):
        number, size = loads[name]
        await_local(load_sem.at[number], size)

    def load_state(t):
        load(f"state {t}", t, (adj.at[t], state.at[t, :, pl.ds(1, ny), body, :]))

    def load_flow(t):
        here = ((vel.at[t], v_buf.at[t]), (grad.at[t], g_buf.at[t]), (heat.at[t], w_buf.at[t]))
        load(f"flow {t}", 5 + t, *here)

    load_state(2)
    load_state(0)

    edge = jnp.zeros((PAD, nz), F32)

    def clear(y, carry):
        for slot in range(state.shape[0]):
            for c in range(4):
                state[slot, c, y, 0:PAD, :] = edge
                state[slot, c, y, PAD + nx : 2 * PAD + nx, :] = edge
        return carry

    lax.fori_loop(0, ny + 2, clear, 0)

    barrier = pltpu.get_barrier_semaphore()
    for other in (before, after, across):
        pl.semaphore_signal(barrier, 1, device_id=(other, tile), device_id_type=MESH)

    @pl.when(has_down)
    def _():
        pl.semaphore_signal(barrier, 1, device_id=(group, tile - 1), device_id_type=MESH)

    @pl.when(has_up)
    def _():
        pl.semaphore_signal(barrier, 1, device_id=(group, tile + 1), device_id_type=MESH)

    @pl.when(via)
    def _():
        pl.semaphore_signal(barrier, 1, device_id=(group, via_from), device_id_type=MESH)

    @pl.when(meets)
    def _():
        for v in vias:
            other = (1 - lower) * v + lower * (tiles - 1 - v)
            pl.semaphore_signal(barrier, 1, device_id=(group, other), device_id_type=MESH)

    extra = via.astype(jnp.int32) + 3 * meets.astype(jnp.int32)
    pl.semaphore_wait(barrier, 3 + has_down.astype(jnp.int32) + has_up.astype(jnp.int32) + extra)

    def encode(slot, y, q, s):
        for c in range(4):
            v = state[slot, c, y + 1, PAD : PAD + nx, :]
            top = jnp.maximum(jnp.max(jnp.abs(v), axis=0, keepdims=True), 1e-30)
            q[c] = jnp.round(v * (TOP / top)).astype(jnp.int32).astype(jnp.int16)
            scale = top * (1.0 / TOP)
            s[c : c + 1, :] = scale
            s[c + 4 : c + 5, :] = scale

    def decode(q, s, slot, row):
        for c in range(4):
            code = q[c].astype(jnp.int32).astype(F32)
            state[slot, c, row, PAD : PAD + nx, :] = code * s[c : c + 1, :]

    def crossing(u, y):
        return [
            pltpu.make_async_remote_copy(
                a.at[u, y], b.at[u, y], x_send.at[0], x_recv.at[u, y],
                device_id=(before, tile), device_id_type=MESH,
            )
            for a, b in ((xs_q, xr_q), (xs_s, xr_s))
        ]

    order = iter([(u, (i + ny - 1) % ny) for u in range(3) for i in range(ny)])

    def cross(u, y):
        for copy in crossing(u, y):
            copy.start()

    def encode_crossing(u, slot, y):
        encode(slot, y, xs_q.at[u, y], xs_s.at[u, y])

    def halo(u, side, q, s):
        other = tile + 1 - 2 * side
        return [
            pltpu.make_async_remote_copy(
                a, b.at[side, u], h_send.at[side], h_recv.at[side, u],
                device_id=(group, other), device_id_type=MESH,
            )
            for a, b in ((q, hr_q), (s, hr_s))
        ]

    def post(u, side, q, s):
        number, scale = halo(u, side, q, s)
        far_apart = tile == (lower_end, upper_end)[side]

        @pl.when(jnp.logical_not(far_apart))
        def _():
            number.start()

        @pl.when(far_apart)
        def _():
            for c, v in enumerate(vias, 1):
                pltpu.make_async_remote_copy(
                    q.at[c], via_q.at[u], h_send.at[side], via_recv.at[u],
                    device_id=(group, (v, tiles - 1 - v)[side]), device_id_type=MESH,
                ).start()
            pltpu.make_async_remote_copy(
                q.at[0], hr_q.at[side, u, 0], h_send.at[side], h_recv.at[side, u],
                device_id=(group, tile + 1 - 2 * side), device_id_type=MESH,
            ).start()

        scale.start()

    def passed_on(u):
        return pltpu.make_async_remote_copy(
            via_q.at[u], hr_q.at[1 - lower, u, via_part], via_send.at[0], h_recv.at[1 - lower, u],
            device_id=(group, via_to), device_id_type=MESH,
        )

    def pass_on(*units):
        @pl.when(via)
        def _():
            for u in units:
                pltpu.make_async_remote_copy(
                    via_q.at[u], via_q.at[u], via_send.at[0], via_recv.at[u],
                    device_id=(group, via_to), device_id_type=MESH,
                ).wait_recv()
                passed_on(u).start()

    def offer(u, slot):
        for side, there, y in ((0, has_up, ny - 1), (1, has_down, 0)):

            @pl.when(there)
            def _():
                encode(slot, y, hs_q.at[side, u], hs_s.at[side, u])
                post(u, side, hs_q.at[side, u], hs_s.at[side, u])

    def relay(u, x):
        for side, there, y in ((0, has_up, ny - 1), (1, has_down, 0)):
            remote_bytes(x_recv.at[x, y], packet).wait_recv()

            @pl.when(there)
            def _():
                post(u, side, xr_q.at[x, y], xr_s.at[x, y])

    def take_halo(u, slot):
        for side, there, row in ((0, has_down, 0), (1, has_up, ny + 1)):

            @pl.when(there)
            def _():
                remote_bytes(h_recv.at[side, u], packet).wait_recv()
                decode(hr_q.at[side, u], hr_s.at[side, u], slot, row)

            @pl.when(jnp.logical_not(there))
            def _():
                for c in range(4):
                    state[slot, c, row, PAD : PAD + nx, :] = jnp.zeros((nx, nz), F32)

    def take_plane(x, slot, y, wait):
        if wait:
            remote_bytes(x_recv.at[x, y], packet).wait_recv()
        decode(xr_q.at[x, y], xr_s.at[x, y], slot, y + 1)

    lane = lax.broadcasted_iota(jnp.int32, (BLOCK, nz), 1)
    not_first, not_last = lane > 0, lane < nz - 1

    def plane(slot, t, y, target, total):
        for x0 in range(0, nx, BLOCK):
            rows = slice(PAD + x0, PAD + x0 + BLOCK)
            left = slice(PAD + x0 - 1, PAD + x0 + BLOCK - 1)
            right = slice(PAD + x0 + 1, PAD + x0 + BLOCK + 1)
            here = slice(x0, x0 + BLOCK)

            def around(c):
                mid = state[slot, c, y + 1, rows, :]
                below = jnp.where(not_first, pltpu.roll(mid, 1, 1), 0.0)
                above = jnp.where(not_last, pltpu.roll(mid, nz - 1, 1), 0.0)
                return (
                    mid, state[slot, c, y + 1, left, :], state[slot, c, y + 1, right, :],
                    state[slot, c, y, rows, :], state[slot, c, y + 2, rows, :], below, above,
                )

            h, xl, xr, yl, yu, zl, zr = around(3)
            speed = [v_buf[t, c, y, here, :].astype(F32) for c in range(3)]
            turn = speed[0] * (xr - xl) + speed[1] * (yu - yl) + speed[2] * (zr - zl)
            ring = (xl + xr) + (yl + yu) + (zl + zr)
            h_new = 0.28 * h + 0.12 * ring + 0.1 * turn + w_buf[t, y, here, :].astype(F32)
            put(target, 3, y, x0, h_new)
            kh = keep[y, here, :] * h
            a, b = cen[y, here, :], nbr[y, here, :]
            term = None
            for c in range(3):
                m, xl, xr, yl, yu, zl, zr = around(c)
                ring = (xl + xr) + (yl + yu) + (zl + zr)
                new = a * m + b * ring - kh * g_buf[t, c, y, here, :].astype(F32)
                put(target, c, y, x0, new)
                if total is not None:
                    term = speed[c] * new if term is None else term + speed[c] * new
            if total == "set":
                acc[y, here, :] = term
            elif total == "add":
                acc[y, here, :] = acc[y, here, :] + term

    def put(target, c, y, x0, value):
        kind_of, number = target
        if kind_of == "fin":
            fin[number % 2, c, y, x0 : x0 + BLOCK, :] = value
        else:
            state[number, c, y + 1, PAD + x0 : PAD + x0 + BLOCK, :] = value

    def out_copy(t, y):
        return pltpu.make_async_copy(fin.at[t % 2, :, y], out.at[t, :, y], out_sem.at[t])

    def chain(slot, t, target, halo_in=None, halo_out=None, cross_out=None, total=None, crosses=0, passes=()):
        due = [next(order) for _ in range(crosses)]

        def one(i, carry):
            for u, at in passes:

                @pl.when(i == at)
                def _(u=u):
                    pass_on(u)

            if halo_in is None:
                y = lax.rem(i + ny - 1, ny)
            else:
                y = lax.rem(i + 1, ny)

                @pl.when(i == ny - 2)
                def _():
                    take_halo(halo_in, slot)

            plane(slot, t, y, target, total)
            if cross_out is not None:
                encode_crossing(cross_out, target[1], y)
            if target[0] == "fin":
                out_copy(t, y).start()
            if halo_out is not None:

                @pl.when(i == (1 if halo_in is None else ny - 1))
                def _():
                    offer(halo_out, target[1])

            for n, (u, plane_of) in enumerate(due):

                @pl.when(i == (3, 6)[n])
                def _(u=u, plane_of=plane_of):
                    cross(u, plane_of)

            return carry

        lax.fori_loop(0, ny, one, 0)

    def written(t):
        pltpu.make_async_copy(fin.at[t % 2], out.at[t], out_sem.at[t]).wait()

    def take_crossing(x, slot):
        def one(i, carry):
            take_plane(x, slot, i, True)
            return carry

        lax.fori_loop(1, ny - 1, one, 0)
        take_plane(x, slot, 0, False)
        take_plane(x, slot, ny - 1, False)

    loaded("state 2")
    load_state(3)
    load_state(1)
    offer(1, 2)
    loaded("state 0")
    load("cells", 4, (density, d_buf), (kind, k_buf), (inlet, i_buf))
    for t in (1, 2, 0, 3):
        load_flow(t)

    def first(i, carry):
        encode_crossing(0, 0, lax.rem(i + ny - 1, ny))

        @pl.when(i == 1)
        def _():
            cross(*next(order))
            cross(*next(order))

        return carry

    lax.fori_loop(0, ny, first, 0)
    for u, t in ((2, 3), (0, 1)):
        loaded(f"state {t}")
        offer(u, t)
    loaded("cells")

    def prepare(y, carry):
        rho = rho_of(d_buf[y], k_buf[y])
        under = 1.0 / (0.5 + rho)
        open_ = (1 - i_buf[y]).astype(F32)
        keep[y] = open_
        nbr[y] = 0.12 * open_
        cen[y] = open_ * (0.28 - 0.25 * (1.0 - rho) * under)
        d_buf[y] = jnp.where(k_buf[y] == 0, -0.375 * under * under, 0.0)
        return carry

    lax.fori_loop(0, ny, prepare, 0)

    def ready(t):
        loaded(f"flow {t}")

    S = "state"
    ready(1)
    chain(2, 1, (S, 5), halo_in=1, halo_out=3, passes=((1, 3), (2, 5), (0, 6)), crosses=2)
    relay(4, 0)
    ready(2)
    take_halo(2, 3)
    chain(3, 2, (S, 2), halo_out=5, passes=((3, 5),), crosses=2)
    ready(0)
    take_halo(0, 1)
    chain(1, 0, (S, 4), cross_out=1, passes=((4, 0), (5, 5)), crosses=2)
    ready(3)
    take_crossing(0, 0)
    take_halo(4, 0)
    chain(0, 3, (S, 1), halo_out=6, crosses=2)
    take_halo(3, 5)
    chain(5, 0, (S, 4), cross_out=2, passes=((6, 5),), crosses=2)
    relay(8, 1)
    take_halo(5, 2)
    chain(2, 1, (S, 3), halo_out=7, passes=((8, 6),), crosses=2)
    take_halo(6, 1)
    chain(1, 2, (S, 5), halo_out=9, passes=((7, 5),), crosses=2)
    take_crossing(1, 0)
    take_halo(8, 0)
    chain(0, 3, (S, 4), halo_out=10, passes=((9, 5),), crosses=2)
    take_halo(7, 3)
    chain(3, 0, ("fin", 0), total="set", passes=((10, 5),), crosses=2)
    relay(11, 2)
    take_halo(9, 5)
    chain(5, 1, ("fin", 1), total="add", passes=((11, 6),), crosses=2)
    written(0)
    take_halo(10, 4)
    chain(4, 2, ("fin", 2), total="add", crosses=2)

    def mine(k):
        return 2 * k + core

    def theirs(k):
        return 2 * k + 1 - core

    def send(n, k, src, dst, other):
        return pltpu.make_async_remote_copy(
            src, dst, s_send.at[0], s_recv.at[n, k], device_id=(other, tile), device_id_type=MESH
        )

    def to_partner(k):
        return send(0, k, acc.at[theirs(k)], near.at[k], partner)

    def to_other_chip(k):
        return send(1, k, half.at[k], far.at[k], across)

    def back(k, y):
        return send(2, k, whole.at[y], whole.at[y], partner)

    def sens_copy(y):
        return pltpu.make_async_copy(whole.at[y], sens.at[y], out_sem.at[4])

    def sum_chip(k):
        to_partner(k).wait_recv()
        half[k] = acc[mine(k)] + near[k]
        to_other_chip(k).start()

    def sum_all(k):
        to_other_chip(k).wait_recv()
        y = mine(k)
        whole[y] = d_buf[y] * (half[k] + far[k])
        back(k, y).start()
        sens_copy(y).start()

    written(1)
    take_halo(11, 0)
    take_plane(2, 0, 0, False)
    take_plane(2, 0, ny - 1, False)

    def last_pair(k, carry):
        @pl.when(k < ny // 2 - 1)
        def _():
            take_plane(2, 0, 2 * k + 1, True)
            take_plane(2, 0, 2 * k + 2, True)

        def one(y, carry):
            plane(0, 3, y, ("fin", 3), "add")
            out_copy(3, y).start()
            return carry

        lax.fori_loop(2 * k, 2 * k + 2, one, 0)
        to_partner(k).start()

        @pl.when(k > 0)
        def _():
            sum_chip(k - 1)

        @pl.when(k > 1)
        def _():
            sum_all(k - 2)

        return carry

    pairs = ny // 2
    lax.fori_loop(0, pairs, last_pair, 0)
    sum_chip(pairs - 1)
    sum_all(pairs - 2)
    sum_all(pairs - 1)
    for k in range(pairs):
        back(k, theirs(k)).wait_recv()
        sens_copy(theirs(k)).start()

    def sent(sem, *refs):
        remote_bytes(sem, tiles_in(*refs)).wait_send()

    sent(s_send.at[0], near, far, half)
    sent(x_send.at[0], xs_q, xs_s)
    for side, there in ((0, has_up), (1, has_down)):

        @pl.when(there)
        def _():
            sent(h_send.at[side], hs_q.at[side], hs_s.at[side])

    @pl.when(via)
    def _():
        sent(via_send.at[0], via_q)

    written(2)
    written(3)
    pltpu.make_async_copy(whole, sens, out_sem.at[4]).wait()


def hand_over(state, total, state_out, total_out, sems):
    phases = state.shape[0]
    copies = [pltpu.make_async_copy(state.at[t], state_out.at[t], sems.at[t]) for t in range(phases)]
    copies.append(pltpu.make_async_copy(total, total_out, sems.at[phases]))
    for copy in copies:
        copy.start()
    for copy in copies:
        copy.wait()


def on_device(tiles, adjoint_in, velocity, temp_grad, heat_weight, density, cell_kind, inlet):
    phases, _, ny, nx, nz = adjoint_in.shape
    bf16, i16, i32 = jnp.bfloat16, jnp.int16, jnp.int32
    vmem, dma = pltpu.VMEM, pltpu.SemaphoreType.DMA
    shapes = (
        jax.ShapeDtypeStruct(adjoint_in.shape, F32),
        jax.ShapeDtypeStruct(density.shape, F32),
    )
    anywhere = pl.BlockSpec(memory_space=pl.ANY)
    results = pl.pallas_call(
        functools.partial(kernel, tiles),
        out_shape=shapes,
        in_specs=[anywhere] * 7,
        out_specs=[anywhere] * 2,
        scratch_shapes=[
            vmem((6, 4, ny + 2, nx + 2 * PAD, nz), F32),
            vmem((2, 4, ny, nx, nz), F32),
            vmem((phases, 3, ny, nx, nz), bf16),
            vmem((phases, 3, ny, nx, nz), bf16),
            vmem((phases, ny, nx, nz), bf16),
            vmem((ny, nx, nz), F32),
            vmem((ny, nx, nz), i32),
            vmem((ny, nx, nz), i32),
            vmem((ny, nx, nz), F32),
            vmem((ny, nx, nz), F32),
            vmem((ny, nx, nz), F32),
            vmem((ny, nx, nz), F32),
            vmem((ny // 2, nx, nz), F32),
            vmem((ny // 2, nx, nz), F32),
            vmem((ny // 2, nx, nz), F32),
            vmem((ny, nx, nz), F32),
            vmem((3, ny, 4, nx, nz), i16),
            vmem((3, ny, 8, nz), F32),
            vmem((3, ny, 4, nx, nz), i16),
            vmem((3, ny, 8, nz), F32),
            vmem((2, 12, 4, nx, nz), i16),
            vmem((2, 12, 8, nz), F32),
            vmem((2, 12, 4, nx, nz), i16),
            vmem((2, 12, 8, nz), F32),
            vmem((12, nx, nz), i16),
            vmem((24 * (8 * nx * nz // TILE + 1), TILE // (4 * nz), nz), F32),
            dma((9,)),
            dma((5,)),
            dma((1,)),
            dma((3, ny)),
            dma((2,)),
            dma((2, 12)),
            dma((1,)),
            dma((3, ny // 2)),
            dma((1,)),
            dma((12,)),
        ],
        compiler_params=pltpu.CompilerParams(
            collective_id=0, has_side_effects=True, vmem_limit_bytes=53 * 2**20
        ),
    )(adjoint_in, velocity, temp_grad, heat_weight, density, cell_kind, inlet)
    return pl.pallas_call(
        hand_over,
        out_shape=shapes,
        in_specs=[anywhere] * 2,
        out_specs=[anywhere] * 2,
        scratch_shapes=[dma((phases + 1,))],
        compiler_params=pltpu.CompilerParams(vmem_limit_bytes=4 * 2**20),
    )(*results)


def solution(mesh):
    return jax.shard_map(
        functools.partial(on_device, mesh.shape["tile"]),
        mesh=mesh,
        in_specs=(
            P("phase", None, "tile", None, None),
            P("phase", None, "tile", None, None),
            P("phase", None, "tile", None, None),
            P("phase", "tile", None, None),
            P("tile", None, None),
            P("tile", None, None),
            P("tile", None, None),
        ),
        out_specs=(P("phase", None, "tile", None, None), P("tile", None, None)),
        check_vma=False,
    )
```
